32 devices in a mesh: groups: 2 (over y), docs: 4 (over z), cent: 2 (over x), sub: 2 (over core).
Axes of the slice: x: 2, y: 2, z: 4, core: 2. Of those that a mesh axis runs over, the one named last changes fastest.
Arguments:
- queries: float32 [256, 128], P(('groups', 'cent', 'sub')), parts along dimension 0, may hold values from -0.6 to 0.6
- token_codes: int32 [4, 256, 8192], P(('cent', 'sub'), ('groups', 'docs')), parts along dimension 1, may hold values from 0 to 255
- centroid_ids: int32 [4, 32768], P(('cent', 'sub'), ('groups', 'docs')), parts along dimension 1, may hold values from 0 to 4095
- slot_counts: int32 [4, 256], P(('cent', 'sub'), ('groups', 'docs')), parts along dimension 1, may hold values from 0 to 128, as said below
- centroids: bfloat16 [16384, 128], P(('cent', 'sub')), may hold values from -3 to 3
- bucket_values: float32 [16, 128], replicated, may hold values from -1.5 to 1.5
- candidates: int32 [8, 64], P(('groups', 'docs')), parts along dimension 0, may hold values from 0 to 127, as said below
- input_proj: float32 [32, 256], replicated, may hold values from -1 to 1
- gain_one: float32 [256], replicated, may hold values from 0.5 to 1.5
- query_proj: bfloat16 [256, 256], replicated, may hold values from -32 to 32, as said below
- key_proj: bfloat16 [256, 256], replicated, may hold values from -1 to 1, as said below
- value_proj: bfloat16 [256, 256], replicated, may hold values from -0.375 to 0.375
- output_proj: bfloat16 [256, 256], replicated, may hold values from -0.375 to 0.375
- gain_two: float32 [256], replicated, may hold values from 0.5 to 1.5
- up_proj: bfloat16 [256, 1024], replicated, may hold values from -0.375 to 0.375
- down_proj: bfloat16 [1024, 256], replicated, may hold values from -0.1875 to 0.1875
Outputs:
- set_states: float32 [8, 64, 256], P(('groups', 'docs'), ('cent', 'sub')), parts along dimension 0
The draws below stay inside these ranges and needn't reach their ends.
There are 2 independent parts, one for each index of `groups`. The reference program is written for one: setup_inputs(seed, part) draws one part's arguments, and reference() takes and returns one part's arrays. A program takes and returns all parts, laid end to end along the dimension named above; an argument that names none is the same for every part. Nothing has to cross between parts.
Inputs may be any that keep to these rules, and one draw needn't show every extreme that they name: `slot_counts`: for every document the counts over the 4 members sum to 256; some member holds 128 live slots of every document. The candidates of one query are distinct. `query_proj`: entries lie within the bounds below. `key_proj`: entries lie within the bounds below.
All inputs are finite; a program needn't handle non-finite values.
Results may differ from the reference program's by a relative error of at most 0.0045.
Values may be sent and summed in bfloat16 or wider, within the bound.
No kernel may reach another device: no remote copies, remote signals or barrier semaphores. Data moves between devices by JAX's collectives and lax.ppermute only.
A program may use at most 64 MiB of HBM per device.

```python
import math
import jax
import jax.numpy as jnp
from jax import lax

DIM = 128
QT = 32
BUCKETS = 16
CENT_DEV = 4096
H = 256
HEADS = 4
FF = 1024
HEAD = 64
NCS = 4
NQ = 4
QROWS = 128
NDOCS = 128
PAD = 128
CAND = 64
NCENT = 16384


def draw_slot_counts(key, part):
    half_pad = PAD // 2

    def one_doc(doc_key):
        device_order = jax.random.permutation(jax.random.fold_in(doc_key, 1), NCS)
        offsets = jax.random.randint(jax.random.fold_in(doc_key, 2), (NCS // 2,), 0, half_pad + 1)
        offsets = offsets.at[0].set(half_pad)
        paired = jnp.stack([half_pad + offsets, half_pad - offsets], axis=1).reshape(NCS)
        return jnp.zeros((NCS,), jnp.int32).at[device_order].set(paired.astype(jnp.int32))
    doc_keys = jax.random.split(jax.random.fold_in(key, 5), NDOCS)
    return jax.vmap(one_doc)(doc_keys).T.astype(jnp.int32)


def draw_candidates(key, part):
    query_keys = jax.random.split(jax.random.fold_in(key, 3), NQ)

    def one_query(query_key):
        return jax.random.permutation(query_key, NDOCS)[:CAND]
    return jax.vmap(one_query)(query_keys).astype(jnp.int32)


def bounded_entries(key):
    unit = jax.random.uniform(key, (H, H), jnp.float32, -1.0, 1.0)
    return unit * math.sqrt(3.0 / H)


def head_factors(key):
    ladder = jnp.exp(jnp.linspace(0.0, math.log(4.0), HEADS)).astype(jnp.float32)
    order = jax.random.permutation(jax.random.fold_in(key, 17), HEADS)
    return jnp.repeat(ladder[order], HEAD)[None, :]


def draw_query_proj(key, part):
    entries = bounded_entries(jax.random.fold_in(key, 7))
    spread_part = 3.0 * entries * head_factors(key)
    return spread_part.astype(jnp.bfloat16)


def draw_key_proj(key, part):
    return bounded_entries(jax.random.fold_in(key, 11)).astype(jnp.bfloat16)


def place_ends(values, rng, smallest, high):
    place = [jax.random.randint(jax.random.fold_in(rng, axis), (), 0, length) for axis, length in enumerate(values.shape)]
    main_axis = values.shape.index(max(values.shape))
    next_to = place[:main_axis] + [(place[main_axis] + 1) % values.shape[main_axis]] + place[main_axis + 1:]
    return values.at[tuple(place)].set(smallest).at[tuple(next_to)].set(high)


def block_levels(stream_key, dims, pieces, smallest, top_value):
    def one(position, shards_of):
        draws = jax.random.uniform(jax.random.fold_in(jax.random.fold_in(stream_key, 6), position), (shards_of,), jnp.float32, smallest / len(pieces), top_value / len(pieces))
        return jnp.repeat(jnp.exp(draws), dims[position] // shards_of).reshape((-1,) + (1,) * (len(dims) - position - 1))

    factor_of = one(*pieces[0])
    for cut in pieces[1:]:
        factor_of = factor_of * one(*cut)
    return factor_of


def scatter_about(stream_key, dims, spread, bound, cuts=(), kind=jnp.bfloat16):
    array = spread * jax.random.normal(stream_key, dims, jnp.float32)
    if cuts:
        array = array * block_levels(stream_key, dims, cuts, -0.22, 0.18)
    return jnp.clip(array, -bound, bound).astype(kind)


def setup_inputs(seed: int = 0, part: int = 0) -> dict:
    splits = jax.random.split(jax.random.key(seed), 17)
    part_keys = jax.random.split(jax.random.fold_in(splits[16], part), 17)
    return {
        "queries": scatter_about(part_keys[0], (QROWS, DIM), 0.1, 0.6, ((0, 4),), jnp.float32),
        "token_codes": place_ends(jax.random.randint(part_keys[1], (NCS, NDOCS, PAD * DIM // 2), 0, 256), jax.random.fold_in(part_keys[1], 1), 0, 255).astype(jnp.int32),
        "centroid_ids": place_ends(jax.random.randint(part_keys[2], (NCS, NDOCS * PAD), 0, CENT_DEV), jax.random.fold_in(part_keys[2], 1), 0, CENT_DEV - 1).astype(jnp.int32),
        "slot_counts": draw_slot_counts(jax.random.fold_in(jax.random.fold_in(splits[16], part), 71), part),
        "centroids": scatter_about(splits[4], (NCENT, DIM), 0.5, 3.0, ((0, 4),)),
        "bucket_values": scatter_about(splits[5], (BUCKETS, DIM), 0.3, 1.5, (), jnp.float32),
        "candidates": draw_candidates(jax.random.fold_in(jax.random.fold_in(splits[16], part), 71), part),
        "input_proj": scatter_about(splits[7], (QT, H), QT ** -0.5, 1.0, (), jnp.float32),
        "gain_one": jnp.clip(1.0 + 0.1 * jax.random.normal(splits[8], (H,), jnp.float32), 0.5, 1.5),
        "query_proj": draw_query_proj(jax.random.fold_in(splits[16], 71), part),
        "key_proj": draw_key_proj(jax.random.fold_in(splits[16], 71), part),
        "value_proj": scatter_about(splits[11], (H, H), H ** -0.5, 0.375),
        "output_proj": scatter_about(splits[12], (H, H), H ** -0.5, 0.375),
        "gain_two": jnp.clip(1.0 + 0.1 * jax.random.normal(splits[13], (H,), jnp.float32), 0.5, 1.5),
        "up_proj": scatter_about(splits[14], (H, FF), H ** -0.5, 0.375),
        "down_proj": scatter_about(splits[15], (FF, H), FF ** -0.5, 0.1875),
    }


def dequantize(code_rows, cent_rows, centroid_table, bucket_table):
    lower = jnp.bitwise_and(code_rows, 15)
    upper = jnp.right_shift(code_rows, 4)
    nibbles = jnp.stack([lower, upper], axis=-1).reshape(code_rows.shape[0], -1)
    residual = jnp.zeros(nibbles.shape, jnp.float32)
    for level_id in range(bucket_table.shape[0]):
        residual = residual + jnp.where(nibbles == level_id, bucket_table[level_id][None, :], jnp.float32(0.0))
    anchor = jnp.take(centroid_table, cent_rows, axis=0).astype(jnp.float32)
    return (anchor + residual).astype(jnp.bfloat16)

def block_maxima(code_rows, cent_rows, live_counts, centroid_table, bucket_table, query_bf, pad_slots):
    embedded = dequantize(code_rows, cent_rows, centroid_table, bucket_table)
    scores = lax.dot_general(embedded, query_bf, (((1,), (1,)), ((), ())), preferred_element_type=jnp.float32)
    positions = jnp.arange(pad_slots, dtype=jnp.int32)
    live_slot = (positions[None, :] < live_counts[:, None]).reshape(-1)
    scores = jnp.where(live_slot[:, None], scores, jnp.float32(-1e+30))
    return lax.optimization_barrier(jnp.max(scores.reshape(live_counts.shape[0], pad_slots, scores.shape[1]), axis=1))

def rms_scale(values, gain):
    mean_square = lax.optimization_barrier(jnp.mean(values * values, axis=-1, keepdims=True))
    return (values * lax.rsqrt(mean_square + 1e-06) * gain).astype(jnp.bfloat16)

def widen(values):
    return lax.optimization_barrier(values).astype(jnp.float32)

def attend(query_heads, key_heads, value_heads):
    rows = query_heads.shape[0]
    query_four = widen(query_heads).reshape(rows, HEADS, HEAD)
    key_four = widen(key_heads).reshape(-1, HEADS, HEAD)
    value_four = widen(value_heads).reshape(-1, HEADS, HEAD)
    scores = jnp.einsum('qhd,khd->hqk', query_four, key_four) * HEAD ** (-0.5)
    peak = lax.optimization_barrier(jnp.max(scores, axis=-1, keepdims=True))
    expon = jnp.exp(scores - peak)
    summed = lax.optimization_barrier(jnp.sum(expon, axis=-1))
    weights = widen(expon.astype(jnp.bfloat16))
    product = jnp.einsum('hqk,khd->qhd', weights, value_four) / summed.T[:, :, None]
    return product.reshape(rows, H).astype(jnp.bfloat16)

def set_layer(features, input_proj, gain_one, query_proj, key_proj, value_proj, output_proj, gain_two, up_proj, down_proj):
    hidden_zero = jnp.dot(features, input_proj, precision=lax.Precision.HIGHEST)
    normed_one = rms_scale(hidden_zero, gain_one)
    query_heads = jnp.dot(normed_one, query_proj, preferred_element_type=jnp.float32).astype(jnp.bfloat16)
    key_heads = jnp.dot(normed_one, key_proj, preferred_element_type=jnp.float32).astype(jnp.bfloat16)
    value_heads = jnp.dot(normed_one, value_proj, preferred_element_type=jnp.float32).astype(jnp.bfloat16)
    attended = attend(query_heads, key_heads, value_heads)
    hidden_one = hidden_zero + jnp.dot(attended, output_proj, preferred_element_type=jnp.float32)
    normed_two = rms_scale(hidden_one, gain_two)
    inner = jax.nn.gelu(jnp.dot(normed_two, up_proj, preferred_element_type=jnp.float32)).astype(jnp.bfloat16)
    return hidden_one + jnp.dot(inner, down_proj, preferred_element_type=jnp.float32)

def reference(queries, token_codes, centroid_ids, slot_counts, centroids, bucket_values, candidates, input_proj, gain_one, query_proj, key_proj, value_proj, output_proj, gain_two, up_proj, down_proj):
    query_bf = queries.astype(jnp.bfloat16)
    block_docs = math.gcd(NDOCS, max(1, 2048 // PAD))
    block_count = NDOCS // block_docs
    code_view = token_codes.reshape(NCS, block_count, block_docs * PAD, DIM // 2)
    cent_view = centroid_ids.reshape(NCS, block_count, block_docs * PAD)
    count_view = slot_counts.reshape(NCS, block_count, block_docs)
    centroid_view = centroids.reshape(NCS, CENT_DEV, DIM)

    def one_block(block_id):
        running_best = jnp.full((block_docs, QROWS), -1e+30, jnp.float32)
        for member in range(NCS):
            running_best = jnp.maximum(running_best, block_maxima(code_view[member, block_id], cent_view[member, block_id], count_view[member, block_id], centroid_view[member], bucket_values, query_bf, PAD))
        return running_best
    maxima = lax.map(one_block, jnp.arange(block_count, dtype=jnp.int32)).reshape(NDOCS, QROWS)
    per_query = maxima.reshape(NDOCS, NQ, QT).transpose(1, 0, 2)
    features = jax.vmap(lambda table, row_ids: jnp.take(table, row_ids, axis=0))(per_query, candidates)

    def one_query(query_features):
        return set_layer(query_features, input_proj, gain_one, query_proj, key_proj, value_proj, output_proj, gain_two, up_proj, down_proj)
    return lax.map(one_query, features)
```

```python
import functools

import jax
import jax.numpy as jnp
from jax import lax
from jax.experimental import pallas as pl
from jax.experimental.pallas import tpu as pltpu
from jax.sharding import PartitionSpec as P

DIM = 128
QT = 32
H = 256
HEADS = 4
HEAD = 64
MEMBERS = ("cent", "sub")
SMALL = 4


def exchange(values, axes):
    width = lax.axis_size(axes)
    if width > SMALL:
        return [lax.all_gather(values, axes, axis=0, tiled=True)]
    pieces = [values]
    for step in range(1, width):
        pieces.append(lax.ppermute(values, axes, [(i, i ^ step) for i in range(width)]))
    return pieces


def place(pieces, out_ref, axes):
    if len(pieces) == 1:
        out_ref[...] = pieces[0][...]
        return
    me = lax.axis_index(axes)
    for step, piece in enumerate(pieces):
        rows = piece.shape[0]
        start = pl.multiple_of(jnp.bitwise_xor(me, step) * rows, rows)
        out_ref[pl.ds(start, rows), :] = piece[...]


def pair_columns(shape, axis):
    wide = lax.broadcasted_iota(jnp.int32, shape, axis)
    dim = lax.broadcasted_iota(jnp.int32, shape, 1 - axis)
    wanted = 2 * jnp.bitwise_and(wide, 63) + jnp.right_shift(wide, 7)
    return jnp.where(wanted == dim, 1.0, 0.0).astype(jnp.bfloat16)


def score_kernel(n_pieces, block, ids, counts, codes, centroids, buckets, *refs):
    pieces, (out_ref, table, anchors, query_all, right) = refs[:n_pieces], refs[n_pieces:]
    docs, columns = codes.shape
    pairs = columns // DIM
    slots = 2 * pairs
    query_rows = query_all.shape[0]

    chunk = 256

    def widen(i, carry):
        start = pl.multiple_of(i * chunk, chunk)
        table[pl.ds(start, chunk), :] = centroids[pl.ds(start, chunk), :].astype(jnp.float32)
        return carry

    lax.fori_loop(0, centroids.shape[0] // chunk, widen, 0)

    def gather(p, carry):
        base = pl.multiple_of(p * docs, docs)
        for n in range(docs):
            row = ids[0, n * slots + p]
            anchors[pl.ds(base + n, 1), :] = table[pl.ds(row, 1), :]
        return carry

    lax.fori_loop(0, slots, gather, 0)

    place(pieces, query_all, MEMBERS)
    query_bf = query_all[...].astype(jnp.bfloat16)
    spread = pair_columns((DIM, 2 * DIM), 1)
    query_pair = jnp.dot(query_bf, spread, preferred_element_type=jnp.float32)
    lane = lax.broadcasted_iota(jnp.int32, (query_rows, 2 * DIM), 1)
    first = jnp.bitwise_and(lane, 64) == 0
    none = jnp.zeros((query_rows, DIM), jnp.bfloat16)
    right[:query_rows, :DIM] = query_bf
    right[:query_rows, DIM : 2 * DIM] = none
    right[:query_rows, 2 * DIM :] = jnp.where(first, query_pair, 0.0).astype(jnp.bfloat16)
    right[query_rows:, :DIM] = none
    right[query_rows:, DIM : 2 * DIM] = query_bf
    right[query_rows:, 2 * DIM :] = jnp.where(first, 0.0, query_pair).astype(jnp.bfloat16)

    levels = jnp.dot(
        buckets[...].astype(jnp.bfloat16), spread, preferred_element_type=jnp.float32
    )
    tables = [[levels[i : i + 8, k : k + DIM] for i in (0, 8)] for k in (0, DIM)]

    def look_up(nibbles, halves):
        index = jnp.bitwise_and(nibbles, 7)
        lower = jnp.take_along_axis(halves[0], index, axis=0)
        upper = jnp.take_along_axis(halves[1], index, axis=0)
        return jnp.where(nibbles >= 8, upper, lower)

    doc_row = lax.broadcasted_iota(jnp.int32, (docs, DIM), 0)
    live = jnp.zeros((docs, DIM), jnp.int32)
    for n in range(docs):
        live = jnp.where(doc_row == n, counts[0, n], live)
    live = jnp.concatenate([live] * (query_rows // DIM), axis=1)

    def score(i, best):
        lefts = []
        for k in range(block):
            pair = i * block + k
            column = pl.multiple_of(pair * DIM, DIM)
            lows, highs = [], []
            for b in range(docs // 8):
                code = codes[b * 8 : b * 8 + 8, pl.ds(column, DIM)]
                lows.append(look_up(jnp.bitwise_and(code, 15), tables[0]))
                highs.append(look_up(jnp.right_shift(code, 4), tables[1]))
            start = pl.multiple_of(pair * (2 * docs), 2 * docs)
            lefts.append(
                jnp.concatenate(
                    [
                        anchors[pl.ds(start, docs), :].astype(jnp.bfloat16),
                        anchors[pl.ds(start + docs, docs), :].astype(jnp.bfloat16),
                        jnp.concatenate(lows, axis=0).astype(jnp.bfloat16),
                        jnp.concatenate(highs, axis=0).astype(jnp.bfloat16),
                    ],
                    axis=1,
                )
            )
        left = jnp.concatenate(lefts, axis=0)
        scores = lax.dot_general(
            left, right[...], (((1,), (1,)), ((), ())), preferred_element_type=jnp.float32
        )
        for k in range(block):
            slot = 2 * (i * block + k)
            rows = scores[k * docs : (k + 1) * docs]
            best = jnp.maximum(best, jnp.where(live > slot, rows[:, :query_rows], -1e30))
            best = jnp.maximum(best, jnp.where(live > slot + 1, rows[:, query_rows:], -1e30))
        return best

    best = jnp.full((docs, query_rows), -1e30, jnp.float32)
    out_ref[...] = lax.fori_loop(0, pairs // block, score, best)


def vmem():
    return pl.BlockSpec(memory_space=pltpu.VMEM)


def smem():
    return pl.BlockSpec(memory_space=pltpu.SMEM)


def local_maxima(ids, counts, codes, centroids, buckets, pieces):
    docs, columns = codes.shape
    query_rows = sum(piece.shape[0] for piece in pieces)
    slots = 2 * columns // DIM
    block = 4
    return pl.pallas_call(
        functools.partial(score_kernel, len(pieces), block),
        out_shape=jax.ShapeDtypeStruct((docs, query_rows), jnp.float32),
        in_specs=[smem(), smem()] + [vmem()] * (3 + len(pieces)),
        out_specs=vmem(),
        scratch_shapes=[
            pltpu.VMEM(centroids.shape, jnp.float32),
            pltpu.VMEM((docs * slots, DIM), jnp.float32),
            pltpu.VMEM((query_rows, DIM), jnp.float32),
            pltpu.VMEM((2 * query_rows, 4 * DIM), jnp.bfloat16),
        ],
        compiler_params=pltpu.CompilerParams(vmem_limit_bytes=40 * 2**20),
        name="local_maxima",
    )(ids, counts, codes, centroids, buckets, *pieces)


def rms_scale(values, gain):
    mean_square = jnp.mean(values * values, axis=-1, keepdims=True)
    return (values * lax.rsqrt(mean_square + 1e-06) * gain).astype(jnp.bfloat16)


def product(left, right):
    return jnp.dot(left, right, preferred_element_type=jnp.float32)


def rerank_kernel(n_pieces, candidates, *refs):
    pieces, refs = refs[:n_pieces], refs[n_pieces:]
    (
        input_proj,
        gain_one,
        query_proj,
        key_proj,
        value_proj,
        output_proj,
        gain_two,
        up_proj,
        down_proj,
        out_ref,
        maxima,
        features,
        first,
        hidden,
        normed,
    ) = refs
    cand = candidates.shape[1]
    rows = out_ref.shape[0]
    place(pieces, maxima, "docs")

    unroll = 32

    def pick(i, carry):
        base = pl.multiple_of(i * unroll, unroll)
        for k in range(unroll):
            features[pl.ds(base + k, 1), :] = maxima[pl.ds(candidates[0, base + k], 1), :]
        return carry

    lax.fori_loop(0, cand // unroll, pick, 0)

    first[...] = jnp.zeros_like(first)
    start = pl.multiple_of(lax.axis_index("docs") * QT, QT)
    first[pl.ds(start, QT), :] = input_proj[...]
    all_hidden = jnp.dot(
        features[...],
        first[...],
        precision=lax.Precision.HIGHEST,
        preferred_element_type=jnp.float32,
    )
    all_normed = rms_scale(all_hidden, gain_one[...])
    hidden[...] = all_hidden
    normed[...] = all_normed
    mine = pl.multiple_of(lax.axis_index(MEMBERS) * rows, rows)
    hidden_zero = hidden[pl.ds(mine, rows), :]
    query_heads = product(normed[pl.ds(mine, rows), :], query_proj[...]).astype(jnp.bfloat16)
    key_heads = product(all_normed, key_proj[...]).astype(jnp.bfloat16)
    value_heads = product(all_normed, value_proj[...]).astype(jnp.bfloat16)
    heads = []
    for h in range(HEADS):
        cut = slice(h * HEAD, (h + 1) * HEAD)
        scores = lax.dot_general(
            query_heads[:, cut],
            key_heads[:, cut],
            (((1,), (1,)), ((), ())),
            preferred_element_type=jnp.float32,
        ) * (HEAD ** (-0.5))
        expon = jnp.exp(scores - jnp.max(scores, axis=-1, keepdims=True))
        summed = jnp.sum(expon, axis=-1, keepdims=True)
        heads.append(product(expon.astype(jnp.bfloat16), value_heads[:, cut]) / summed)
    attended = jnp.concatenate(heads, axis=1).astype(jnp.bfloat16)
    hidden_one = hidden_zero + product(attended, output_proj[...])
    normed_two = rms_scale(hidden_one, gain_two[...])
    inner = jax.nn.gelu(product(normed_two, up_proj[...])).astype(jnp.bfloat16)
    out_ref[...] = hidden_one + product(inner, down_proj[...])


def rerank(candidates, pieces, weights, rows):
    docs_all = sum(piece.shape[0] for piece in pieces)
    query_rows = pieces[0].shape[1]
    cand = candidates.shape[1]
    return pl.pallas_call(
        functools.partial(rerank_kernel, len(pieces)),
        out_shape=jax.ShapeDtypeStruct((rows, H), jnp.float32),
        in_specs=[smem()] + [vmem()] * (len(pieces) + len(weights)),
        out_specs=vmem(),
        scratch_shapes=[
            pltpu.VMEM((docs_all, query_rows), jnp.float32),
            pltpu.VMEM((cand, query_rows), jnp.float32),
            pltpu.VMEM((query_rows, H), jnp.float32),
            pltpu.VMEM((cand, H), jnp.float32),
            pltpu.VMEM((cand, H), jnp.bfloat16),
        ],
        compiler_params=pltpu.CompilerParams(vmem_limit_bytes=40 * 2**20),
        name="rerank",
    )(candidates, *pieces, *weights)


def on_device(
    queries,
    token_codes,
    centroid_ids,
    slot_counts,
    centroids,
    bucket_values,
    candidates,
    input_proj,
    gain_one,
    query_proj,
    key_proj,
    value_proj,
    output_proj,
    gain_two,
    up_proj,
    down_proj,
):
    query_pieces = exchange(queries, MEMBERS)
    local_best = local_maxima(
        centroid_ids, slot_counts, token_codes[0], centroids, bucket_values, query_pieces
    )
    if lax.axis_size(MEMBERS) > SMALL:
        doc_best = lax.pmax(local_best, MEMBERS)
    else:
        doc_best = functools.reduce(jnp.maximum, exchange(local_best, MEMBERS))
    doc_pieces = exchange(doc_best, "docs")
    rows = candidates.shape[1] // lax.axis_size(MEMBERS)
    weights = (
        input_proj,
        gain_one[None, :],
        query_proj,
        key_proj,
        value_proj,
        output_proj,
        gain_two[None, :],
        up_proj,
        down_proj,
    )
    return rerank(candidates, doc_pieces, weights, rows)[None]


def solution(mesh):
    in_specs = (
        P(("groups", "cent", "sub"), None),
        P(("cent", "sub"), ("groups", "docs"), None),
        P(("cent", "sub"), ("groups", "docs")),
        P(("cent", "sub"), ("groups", "docs")),
        P(("cent", "sub"), None),
        P(),
        P(("groups", "docs"), None),
        P(),
        P(),
        P(),
        P(),
        P(),
        P(),
        P(),
        P(),
        P(),
    )
    out_specs = P(("groups", "docs"), ("cent", "sub"), None)
    return jax.shard_map(
        on_device, mesh=mesh, in_specs=in_specs, out_specs=out_specs, check_vma=False
    )
```

```python
import functools

import jax
import jax.numpy as jnp
from jax import lax
from jax.experimental import pallas as pl
from jax.experimental.pallas import tpu as pltpu
from jax.sharding import PartitionSpec as P

DIM = 128
QT = 32
H = 256
HEADS = 4
HEAD = 64
MEMBERS = ("cent", "sub")
NOTHING = -1e30
DOC_STEPS = ((2, 3, 1, 0), (3, 2, 0, 1), (1, 0, 3, 2))


def compact():
    return (
        lax.axis_size("cent") == 2
        and lax.axis_size("sub") == 2
        and lax.axis_size("docs") == len(DOC_STEPS) + 1
    )


def gather_queries(queries):
    if not compact():
        return [lax.all_gather(queries, MEMBERS, axis=0, tiled=True)], [None]
    pieces, sources = [queries], [[0, 1, 2, 3]]
    for step in (1, 2, 3):
        sources.append([i ^ step for i in range(4)])
        pieces.append(lax.ppermute(queries, MEMBERS, [(i, i ^ step) for i in range(4)]))
    return pieces, sources


def best_of_members(values):
    if not compact():
        return lax.pmax(values, MEMBERS)
    values = jnp.maximum(values, lax.ppermute(values, "sub", [(0, 1), (1, 0)]))
    return jnp.maximum(values, lax.ppermute(values, MEMBERS, [(i, i ^ 3) for i in range(4)]))


def gather_docs(values):
    if not compact():
        return [lax.all_gather(values, "docs", axis=0, tiled=True)], [None]
    pieces, sources = [values], [[0, 1, 2, 3]]
    for step in reversed(DOC_STEPS):
        pairs = [(2 * d + c, 2 * step[d] + 1 - c) for d in range(4) for c in range(2)]
        pieces.append(lax.ppermute(values, ("docs", "sub"), pairs))
        sources.append([step.index(d) for d in range(4)])
    return pieces, sources


def place(pieces, sources, out_ref, axes):
    if len(pieces) == 1:
        out_ref[...] = pieces[0][...]
        return
    me = lax.axis_index(axes)
    for piece, source in zip(pieces, sources):
        rows = piece.shape[0]
        place_of = jnp.int32(source[0])
        for i in range(1, len(source)):
            place_of = jnp.where(me == i, source[i], place_of)
        start = pl.multiple_of(place_of * rows, rows)
        out_ref[pl.ds(start, rows), :] = piece[...]


def vmem():
    return pl.BlockSpec(memory_space=pltpu.VMEM)


def smem():
    return pl.BlockSpec(memory_space=pltpu.SMEM)


def hbm():
    return pl.BlockSpec(memory_space=pltpu.HBM)


def in_hbm(array):
    return pltpu.with_memory_space_constraint(array, pltpu.HBM)


def even_odd_columns():
    wide = lax.broadcasted_iota(jnp.int32, (DIM, 2 * DIM), 1)
    dim = lax.broadcasted_iota(jnp.int32, (DIM, 2 * DIM), 0)
    wanted = 2 * jnp.bitwise_and(wide, 63) + jnp.right_shift(wide, 7)
    return jnp.where(wanted == dim, 1.0, 0.0).astype(jnp.bfloat16)


def look_up(nibbles, halves):
    index = jnp.bitwise_and(nibbles, 7)
    lower = jnp.take_along_axis(halves[0], index, axis=0)
    upper = jnp.take_along_axis(halves[1], index, axis=0)
    return jnp.where(nibbles >= 8, upper, lower)


def prepare_kernel(n_kept, ids_hbm, counts_hbm, codes_hbm, centroids_hbm, buckets_hbm, *refs):
    kept_hbm, refs = refs[:n_kept], refs[n_kept:]
    left, live, spread = refs[:3]
    kept, refs = refs[3 : 3 + n_kept], refs[3 + n_kept :]
    ids, counts, codes, centroids, buckets, table, anchors, sems, kept_sems = refs
    docs, columns = codes.shape
    pairs = columns // DIM
    slots = 2 * pairs

    copies = [
        pltpu.make_async_copy(source, target, sems.at[i])
        for i, (source, target) in enumerate(
            (
                (centroids_hbm, centroids),
                (ids_hbm, ids),
                (buckets_hbm, buckets),
                (counts_hbm, counts),
                (codes_hbm, codes),
            )
        )
    ]
    copies += [
        pltpu.make_async_copy(source, target, kept_sems.at[i])
        for i, (source, target) in enumerate(zip(kept_hbm, kept))
    ]
    for copy in copies:
        copy.start()
    columns_of = even_odd_columns()
    spread[...] = columns_of

    copies[2].wait()
    levels = jnp.dot(
        buckets[...].astype(jnp.bfloat16), columns_of, preferred_element_type=jnp.float32
    )
    tables = [[levels[i : i + 8, k : k + DIM] for i in (0, 8)] for k in (0, DIM)]

    copies[0].wait()
    chunk = 512

    def widen(i, carry):
        start = pl.multiple_of(i * chunk, chunk)
        table[pl.ds(start, chunk), :] = centroids[pl.ds(start, chunk), :].astype(jnp.float32)
        return carry

    lax.fori_loop(0, centroids.shape[0] // chunk, widen, 0)

    copies[1].wait()
    copies[3].wait()
    doc_row = lax.broadcasted_iota(jnp.int32, (8, DIM), 0)
    for b in range(docs // 8):
        block = jnp.zeros((8, DIM), jnp.int32)
        for n in range(8):
            block = jnp.where(doc_row == n, counts[0, b * 8 + n], block)
        live[b * 8 : b * 8 + 8, :] = block

    copies[4].wait()
    for pair in range(pairs):
        start = pair * docs
        for k in range(2):

            def fetch(n, carry, first=2 * start + k * docs, slot=2 * pair + k):
                row = ids[0, n * slots + slot]
                anchors[pl.ds(first + n, 1), :] = table[pl.ds(row, 1), :]
                return carry

            lax.fori_loop(0, docs, fetch, 0, unroll=True)
        lows, highs = [], []
        for b in range(docs // 8):
            code = codes[b * 8 : b * 8 + 8, pair * DIM : (pair + 1) * DIM]
            lows.append(look_up(jnp.bitwise_and(code, 15), tables[0]))
            highs.append(look_up(jnp.right_shift(code, 4), tables[1]))
        rows = slice(start, start + docs)
        left[rows, 2 * DIM : 3 * DIM] = jnp.concatenate(lows, axis=0).astype(jnp.bfloat16)
        left[rows, 3 * DIM :] = jnp.concatenate(highs, axis=0).astype(jnp.bfloat16)
        for k in range(2):
            found = anchors[2 * start + k * docs : 2 * start + (k + 1) * docs, :]
            left[rows, k * DIM : (k + 1) * DIM] = found.astype(jnp.bfloat16)
    for copy in copies[5:]:
        copy.wait()


def prepare(ids, counts, codes, centroids, buckets, kept):
    docs, columns = codes.shape
    pairs = columns // DIM
    shape = jax.ShapeDtypeStruct
    return pl.pallas_call(
        functools.partial(prepare_kernel, len(kept)),
        out_shape=[
            shape((pairs * docs, 4 * DIM), jnp.bfloat16),
            shape((docs, DIM), jnp.int32),
            shape((DIM, 2 * DIM), jnp.bfloat16),
        ]
        + [shape(array.shape, array.dtype) for array in kept],
        in_specs=[hbm()] * (5 + len(kept)),
        out_specs=[vmem()] * (3 + len(kept)),
        scratch_shapes=[
            pltpu.SMEM(ids.shape, jnp.int32),
            pltpu.SMEM(counts.shape, jnp.int32),
            pltpu.VMEM(codes.shape, jnp.int32),
            pltpu.VMEM(centroids.shape, jnp.bfloat16),
            pltpu.VMEM(buckets.shape, jnp.float32),
            pltpu.VMEM(centroids.shape, jnp.float32),
            pltpu.VMEM((2 * pairs * docs, DIM), jnp.float32),
            pltpu.SemaphoreType.DMA((5,)),
            pltpu.SemaphoreType.DMA((len(kept),)),
        ],
        compiler_params=pltpu.CompilerParams(vmem_limit_bytes=24 * 2**20),
        cost_estimate=pl.CostEstimate(flops=4 * 10**9, bytes_accessed=2**22, transcendentals=0),
        name="prepare",
    )(*[in_hbm(x) for x in (ids, counts, codes, centroids, buckets, *kept)])


def score_kernel(sources, docs, left, live, spread, *refs):
    pieces, (out_ref, queries, right) = refs[: len(sources)], refs[len(sources) :]
    query_rows = queries.shape[0]
    pairs = left.shape[0] // docs
    place(pieces, sources, queries, MEMBERS)
    query_bf = queries[...].astype(jnp.bfloat16)
    query_pair = jnp.dot(query_bf, spread[...], preferred_element_type=jnp.float32)
    lane = lax.broadcasted_iota(jnp.int32, (query_rows, 2 * DIM), 1)
    first = jnp.bitwise_and(lane, 64) == 0
    none = jnp.zeros((query_rows, DIM), jnp.bfloat16)
    right[:query_rows, :DIM] = query_bf
    right[:query_rows, DIM : 2 * DIM] = none
    right[:query_rows, 2 * DIM :] = jnp.where(first, query_pair, 0.0).astype(jnp.bfloat16)
    right[query_rows:, :DIM] = none
    right[query_rows:, DIM : 2 * DIM] = query_bf
    right[query_rows:, 2 * DIM :] = jnp.where(first, 0.0, query_pair).astype(jnp.bfloat16)

    counts = jnp.concatenate([live[...]] * (query_rows // DIM), axis=1)
    block = pairs if query_rows == DIM else 4

    def score(i, best):
        start = pl.multiple_of(i * block * docs, block * docs)
        scores = lax.dot_general(
            left[pl.ds(start, block * docs), :],
            right[...],
            (((1,), (1,)), ((), ())),
            preferred_element_type=jnp.float32,
        )
        for k in range(block):
            slot = 2 * (i * block + k)
            rows = scores[k * docs : (k + 1) * docs]
            best = jnp.maximum(best, jnp.where(counts > slot, rows[:, :query_rows], NOTHING))
            best = jnp.maximum(best, jnp.where(counts > slot + 1, rows[:, query_rows:], NOTHING))
        return best

    best = jnp.full((docs, query_rows), NOTHING, jnp.float32)
    if block == pairs:
        out_ref[...] = score(0, best)
    else:
        out_ref[...] = lax.fori_loop(0, pairs // block, score, best)


def local_maxima(left, live, spread, pieces, sources):
    docs = live.shape[0]
    query_rows = sum(piece.shape[0] for piece in pieces)
    return pl.pallas_call(
        functools.partial(score_kernel, sources, docs),
        out_shape=jax.ShapeDtypeStruct((docs, query_rows), jnp.float32),
        in_specs=[vmem()] * (3 + len(pieces)),
        out_specs=vmem(),
        scratch_shapes=[
            pltpu.VMEM((query_rows, DIM), jnp.float32),
            pltpu.VMEM((2 * query_rows, 4 * DIM), jnp.bfloat16),
        ],
        compiler_params=pltpu.CompilerParams(vmem_limit_bytes=24 * 2**20),
        name="local_maxima",
    )(left, live, spread, *pieces)


def rms_scale(values, gain):
    mean_square = jnp.mean(values * values, axis=-1, keepdims=True)
    return (values * lax.rsqrt(mean_square + 1e-06) * gain).astype(jnp.bfloat16)


def product(left, right):
    return jnp.dot(left, right, preferred_element_type=jnp.float32)


def rerank_kernel(sources, *refs):
    pieces, refs = refs[: len(sources)], refs[len(sources) :]
    (
        candidates,
        input_proj,
        gain_one,
        query_proj,
        key_proj,
        value_proj,
        output_proj,
        gain_two,
        up_proj,
        down_proj,
        out_ref,
        maxima,
        first,
        hidden,
        normed,
    ) = refs
    cand = candidates.shape[1]
    rows = out_ref.shape[0]
    place(pieces, sources, maxima, "docs")

    doc = lax.broadcasted_iota(jnp.int32, (maxima.shape[0], cand), 0)
    chosen = jnp.where(doc == candidates[...], 1.0, 0.0).astype(jnp.bfloat16)
    rest = maxima[...]
    features = None
    for _ in range(3):
        part = rest.astype(jnp.bfloat16)
        rest = rest - part.astype(jnp.float32)
        taken = lax.dot_general(
            chosen, part, (((0,), (0,)), ((), ())), preferred_element_type=jnp.float32
        )
        features = taken if features is None else features + taken

    first[...] = jnp.zeros_like(first)
    start = pl.multiple_of(lax.axis_index("docs") * QT, QT)
    first[pl.ds(start, QT), :] = input_proj[...]
    all_hidden = jnp.dot(
        features,
        first[...],
        precision=lax.Precision.HIGHEST,
        preferred_element_type=jnp.float32,
    )
    all_normed = rms_scale(all_hidden, gain_one[...])
    hidden[...] = all_hidden
    normed[...] = all_normed
    mine = pl.multiple_of(lax.axis_index(MEMBERS) * rows, rows)
    hidden_zero = hidden[pl.ds(mine, rows), :]
    query_heads = product(normed[pl.ds(mine, rows), :], query_proj[...]).astype(jnp.bfloat16)
    key_heads = product(all_normed, key_proj[...]).astype(jnp.bfloat16)
    value_heads = product(all_normed, value_proj[...]).astype(jnp.bfloat16)

    head_of = jnp.right_shift(lax.broadcasted_iota(jnp.int32, (rows, H), 1), 6)
    split = [jnp.where(head_of == h, query_heads, jnp.zeros_like(query_heads)) for h in range(HEADS)]
    scores = lax.dot_general(
        jnp.concatenate(split, axis=0),
        key_heads,
        (((1,), (1,)), ((), ())),
        preferred_element_type=jnp.float32,
    ) * (HEAD ** (-0.5))
    expon = jnp.exp(scores - jnp.max(scores, axis=-1, keepdims=True))
    summed = jnp.sum(expon, axis=-1, keepdims=True)
    spread = product(expon.astype(jnp.bfloat16), value_heads) / summed
    attended = spread[:rows]
    for h in range(1, HEADS):
        attended = jnp.where(head_of == h, spread[h * rows : (h + 1) * rows], attended)
    hidden_one = hidden_zero + product(attended.astype(jnp.bfloat16), output_proj[...])
    normed_two = rms_scale(hidden_one, gain_two[...])
    inner = jax.nn.gelu(product(normed_two, up_proj[...])).astype(jnp.bfloat16)
    out_ref[...] = hidden_one + product(inner, down_proj[...])


def rerank(pieces, sources, arrays, rows):
    docs_all = sum(piece.shape[0] for piece in pieces)
    query_rows = pieces[0].shape[1]
    cand = arrays[0].shape[1]
    return pl.pallas_call(
        functools.partial(rerank_kernel, sources),
        out_shape=jax.ShapeDtypeStruct((rows, H), jnp.float32),
        in_specs=[vmem()] * (len(pieces) + len(arrays)),
        out_specs=vmem(),
        scratch_shapes=[
            pltpu.VMEM((docs_all, query_rows), jnp.float32),
            pltpu.VMEM((query_rows, H), jnp.float32),
            pltpu.VMEM((cand, H), jnp.float32),
            pltpu.VMEM((cand, H), jnp.bfloat16),
        ],
        compiler_params=pltpu.CompilerParams(vmem_limit_bytes=32 * 2**20),
        name="rerank",
    )(*pieces, *arrays)


def on_device(
    queries,
    token_codes,
    centroid_ids,
    slot_counts,
    centroids,
    bucket_values,
    candidates,
    input_proj,
    gain_one,
    query_proj,
    key_proj,
    value_proj,
    output_proj,
    gain_two,
    up_proj,
    down_proj,
):
    kept = (
        candidates,
        input_proj,
        gain_one[None, :],
        query_proj,
        key_proj,
        value_proj,
        output_proj,
        gain_two[None, :],
        up_proj,
        down_proj,
    )
    query_pieces, query_sources = gather_queries(queries)
    left, live, spread, *kept = prepare(
        centroid_ids, slot_counts, token_codes[0], centroids, bucket_values, kept
    )
    local_best = local_maxima(left, live, spread, query_pieces, query_sources)
    doc_pieces, doc_sources = gather_docs(best_of_members(local_best))
    rows = candidates.shape[1] // lax.axis_size(MEMBERS)
    return rerank(doc_pieces, doc_sources, kept, rows)[None]


def solution(mesh):
    in_specs = (
        P(("groups", "cent", "sub"), None),
        P(("cent", "sub"), ("groups", "docs"), None),
        P(("cent", "sub"), ("groups", "docs")),
        P(("cent", "sub"), ("groups", "docs")),
        P(("cent", "sub"), None),
        P(),
        P(("groups", "docs"), None),
        P(),
        P(),
        P(),
        P(),
        P(),
        P(),
        P(),
        P(),
        P(),
    )
    out_specs = P(("groups", "docs"), ("cent", "sub"), None)
    return jax.shard_map(
        on_device, mesh=mesh, in_specs=in_specs, out_specs=out_specs, check_vma=False
    )
```

```python
import functools

import jax
import jax.numpy as jnp
from jax import lax
from jax.experimental import pallas as pl
from jax.experimental.pallas import tpu as pltpu
from jax.sharding import PartitionSpec as P

DIM = 128
QT = 32
H = 256
HEADS = 4
HEAD = 64
MEMBERS = ("cent", "sub")
NOTHING = -1e30
CHUNKS = 4
PART_PAIRS = ((0, 0), (0, 1), (0, 2), (1, 0), (1, 1), (2, 0))
DOC_STEPS = ((2, 3, 1, 0), (3, 2, 0, 1), (1, 0, 3, 2))


def compact():
    return (
        lax.axis_size("cent") == 2
        and lax.axis_size("sub") == 2
        and lax.axis_size("docs") == len(DOC_STEPS) + 1
    )


def gather_queries(queries):
    if not compact():
        return [lax.all_gather(queries, MEMBERS, axis=0, tiled=True)], [None]
    pieces, sources = [queries], [[0, 1, 2, 3]]
    for step in (1, 2, 3):
        sources.append([i ^ step for i in range(4)])
        pieces.append(lax.ppermute(queries, MEMBERS, [(i, i ^ step) for i in range(4)]))
    return pieces, sources


def best_of_members(values):
    if not compact():
        return lax.pmax(values, MEMBERS)
    values = jnp.maximum(values, lax.ppermute(values, "sub", [(0, 1), (1, 0)]))
    return jnp.maximum(values, lax.ppermute(values, MEMBERS, [(i, i ^ 3) for i in range(4)]))


def gather_docs(values):
    if not compact():
        return [lax.all_gather(values, "docs", axis=0, tiled=True)], [None]
    pieces, sources = [values], [[0, 1, 2, 3]]
    for step in reversed(DOC_STEPS):
        pairs = [(2 * d + c, 2 * step[d] + 1 - c) for d in range(4) for c in range(2)]
        pieces.append(lax.ppermute(values, ("docs", "sub"), pairs))
        sources.append([step.index(d) for d in range(4)])
    return pieces, sources


def place(pieces, sources, out_ref, axes):
    if len(pieces) == 1:
        out_ref[...] = pieces[0][...]
        return
    me = lax.axis_index(axes)
    for piece, source in zip(pieces, sources):
        rows = piece.shape[0]
        place_of = jnp.int32(source[0])
        for i in range(1, len(source)):
            place_of = jnp.where(me == i, source[i], place_of)
        start = pl.multiple_of(place_of * rows, rows)
        out_ref[pl.ds(start, rows), :] = piece[...]


def vmem():
    return pl.BlockSpec(memory_space=pltpu.VMEM)


def smem():
    return pl.BlockSpec(memory_space=pltpu.SMEM)


def hbm():
    return pl.BlockSpec(memory_space=pltpu.HBM)


def in_hbm(array):
    return pltpu.with_memory_space_constraint(array, pltpu.HBM)


def even_odd_columns():
    wide = lax.broadcasted_iota(jnp.int32, (DIM, 2 * DIM), 1)
    dim = lax.broadcasted_iota(jnp.int32, (DIM, 2 * DIM), 0)
    wanted = 2 * jnp.bitwise_and(wide, 63) + jnp.right_shift(wide, 7)
    return jnp.where(wanted == dim, 1.0, 0.0).astype(jnp.bfloat16)


def three_parts(values):
    parts = []
    for _ in range(3):
        part = values.astype(jnp.bfloat16)
        values = values - part.astype(jnp.float32)
        parts.append(part)
    return parts


def look_up(nibbles, halves):
    index = jnp.bitwise_and(nibbles, 7)
    lower = jnp.take_along_axis(halves[0], index, axis=0)
    upper = jnp.take_along_axis(halves[1], index, axis=0)
    return jnp.where(nibbles >= 8, upper, lower)


def prepare_kernel(n_kept, *refs):
    ids_hbm, counts_hbm, candidates_hbm, codes_hbm, centroids_hbm, buckets_hbm, proj_hbm = refs[:7]
    kept_hbm, refs = refs[7 : 7 + n_kept], refs[7 + n_kept :]
    left, live, spread, chosen, proj_parts = refs[:5]
    kept, refs = refs[5 : 5 + n_kept], refs[5 + n_kept :]
    ids, counts, candidates, codes, centroids, buckets, proj, table, sems, chunk_sems, code_sems, kept_sems = refs
    docs, columns = codes.shape
    pairs = columns // DIM
    slots = 2 * pairs
    cand = candidates.shape[1]
    rows_dev = chosen.shape[0] - cand

    chunk = centroids.shape[0] // CHUNKS
    chunks = [
        pltpu.make_async_copy(
            centroids_hbm.at[pl.ds(i * chunk, chunk), :],
            centroids.at[pl.ds(i * chunk, chunk), :],
            chunk_sems.at[i],
        )
        for i in range(CHUNKS)
    ]
    small = [
        pltpu.make_async_copy(source, target, sems.at[i])
        for i, (source, target) in enumerate(
            (
                (ids_hbm, ids),
                (buckets_hbm, buckets),
                (counts_hbm, counts),
                (candidates_hbm, candidates),
                (proj_hbm, proj),
            )
        )
    ]
    part = columns // CHUNKS
    code_chunks = [
        pltpu.make_async_copy(
            codes_hbm.at[:, pl.ds(i * part, part)],
            codes.at[:, pl.ds(i * part, part)],
            code_sems.at[i],
        )
        for i in range(CHUNKS)
    ]
    late = [
        pltpu.make_async_copy(source, target, kept_sems.at[i])
        for i, (source, target) in enumerate(zip(kept_hbm, kept))
    ]
    for copy in small + chunks + code_chunks:
        copy.start()
    columns_of = even_odd_columns()
    spread[...] = columns_of

    small[1].wait()
    levels = jnp.dot(
        buckets[...].astype(jnp.bfloat16), columns_of, preferred_element_type=jnp.float32
    )
    tables = [[levels[i : i + 8, k : k + DIM] for i in (0, 8)] for k in (0, DIM)]
    small[2].wait()
    doc_row = lax.broadcasted_iota(jnp.int32, (8, DIM), 0)
    for b in range(docs // 8):
        block = jnp.zeros((8, DIM), jnp.int32)
        for n in range(8):
            block = jnp.where(doc_row == n, counts[0, b * 8 + n], block)
        live[b * 8 : b * 8 + 8, :] = block

    small[3].wait()
    docs_all = chosen.shape[1]
    member = lax.axis_index(MEMBERS)
    doc = lax.broadcasted_iota(jnp.int32, (16, docs_all), 1)
    place_in = lax.broadcasted_iota(jnp.int32, (16, docs_all), 0)

    def choose(i, carry):
        start = pl.multiple_of(i * 16, 16)
        source = jnp.where(start < cand, start, start - cand + member * rows_dev)
        wanted = jnp.zeros((16, docs_all), jnp.int32)
        for n in range(16):
            wanted = jnp.where(place_in == n, candidates[0, source + n], wanted)
        chosen[pl.ds(start, 16), :] = jnp.where(doc == wanted, 1.0, 0.0).astype(jnp.bfloat16)
        return carry

    lax.fori_loop(0, chosen.shape[0] // 16, choose, 0)
    small[4].wait()
    parts = three_parts(proj[...])
    for i, k in enumerate(PART_PAIRS):
        proj_parts[i * QT : (i + 1) * QT, :] = parts[k[1]]

    for i, copy in enumerate(chunks):
        copy.wait()
        for first in range(i * chunk, (i + 1) * chunk, 256):
            table[first : first + 256, :] = centroids[first : first + 256, :].astype(jnp.float32)
    small[0].wait()
    row_bits = [jnp.bitwise_and(doc_row, bit) != 0 for bit in (1, 2, 4)]

    def fetch(slot, first):
        rows = []
        for n in range(first, first + 8):
            row = table[pl.ds(ids[0, n * slots + slot], 1), :]
            rows.append(jnp.broadcast_to(row, (8, DIM)))
        for bit in row_bits:
            rows = [jnp.where(bit, rows[i + 1], rows[i]) for i in range(0, len(rows), 2)]
        return rows[0]

    def one_pair(pair, carry):
        start = pl.multiple_of(pair * docs, docs)
        column = pl.multiple_of(pair * DIM, DIM)
        parts = [[], [], [], []]
        for b in range(0, docs, 8):
            code = codes[b : b + 8, pl.ds(column, DIM)]
            parts[0].append(fetch(2 * pair, b))
            parts[1].append(fetch(2 * pair + 1, b))
            parts[2].append(look_up(jnp.bitwise_and(code, 15), tables[0]))
            parts[3].append(look_up(jnp.right_shift(code, 4), tables[1]))
        for k, part in enumerate(parts):
            columns = slice(k * DIM, (k + 1) * DIM)
            left[pl.ds(start, docs), columns] = jnp.concatenate(part, axis=0).astype(jnp.bfloat16)
        return carry

    for i, copy in enumerate(code_chunks):
        copy.wait()
        if i == 1:
            for other in late:
                other.start()
        lax.fori_loop(
            i * pairs // CHUNKS, (i + 1) * pairs // CHUNKS, one_pair, 0, unroll=True
        )
    for copy in late:
        copy.wait()


def prepare(ids, counts, candidates, codes, centroids, buckets, input_proj, docs_all, rows, kept):
    docs, columns = codes.shape
    pairs = columns // DIM
    shape = jax.ShapeDtypeStruct
    return pl.pallas_call(
        functools.partial(prepare_kernel, len(kept)),
        out_shape=[
            shape((pairs * docs, 4 * DIM), jnp.bfloat16),
            shape((docs, DIM), jnp.int32),
            shape((DIM, 2 * DIM), jnp.bfloat16),
            shape((candidates.shape[1] + rows, docs_all), jnp.bfloat16),
            shape((len(PART_PAIRS) * QT, H), jnp.bfloat16),
        ]
        + [shape(array.shape, array.dtype) for array in kept],
        in_specs=[hbm()] * (7 + len(kept)),
        out_specs=[vmem()] * (5 + len(kept)),
        scratch_shapes=[
            pltpu.SMEM(ids.shape, jnp.int32),
            pltpu.SMEM(counts.shape, jnp.int32),
            pltpu.SMEM(candidates.shape, jnp.int32),
            pltpu.VMEM(codes.shape, jnp.int32),
            pltpu.VMEM(centroids.shape, jnp.bfloat16),
            pltpu.VMEM(buckets.shape, jnp.float32),
            pltpu.VMEM(input_proj.shape, jnp.float32),
            pltpu.VMEM(centroids.shape, jnp.float32),
            pltpu.SemaphoreType.DMA((5,)),
            pltpu.SemaphoreType.DMA((CHUNKS,)),
            pltpu.SemaphoreType.DMA((CHUNKS,)),
            pltpu.SemaphoreType.DMA((len(kept),)),
        ],
        compiler_params=pltpu.CompilerParams(vmem_limit_bytes=24 * 2**20),
        cost_estimate=pl.CostEstimate(flops=4 * 10**9, bytes_accessed=2**22, transcendentals=0),
        name="prepare",
    )(
        *[
            in_hbm(x)
            for x in (ids, counts, candidates, codes, centroids, buckets, input_proj, *kept)
        ]
    )


def score_kernel(sources, docs, left, live, spread, *refs):
    pieces, (out_ref, queries, right) = refs[: len(sources)], refs[len(sources) :]
    query_rows = queries.shape[0]
    pairs = left.shape[0] // docs
    place(pieces, sources, queries, MEMBERS)
    query_bf = queries[...].astype(jnp.bfloat16)
    query_pair = jnp.dot(query_bf, spread[...], preferred_element_type=jnp.float32)
    lane = lax.broadcasted_iota(jnp.int32, (query_rows, 2 * DIM), 1)
    first = jnp.bitwise_and(lane, 64) == 0
    none = jnp.zeros((query_rows, DIM), jnp.bfloat16)
    right[:query_rows, :DIM] = query_bf
    right[:query_rows, DIM : 2 * DIM] = none
    right[:query_rows, 2 * DIM :] = jnp.where(first, query_pair, 0.0).astype(jnp.bfloat16)
    right[query_rows:, :DIM] = none
    right[query_rows:, DIM : 2 * DIM] = query_bf
    right[query_rows:, 2 * DIM :] = jnp.where(first, 0.0, query_pair).astype(jnp.bfloat16)

    counts = jnp.concatenate([live[...]] * (query_rows // DIM), axis=1)
    block = pairs if query_rows == DIM else 4

    def score(i, best):
        start = pl.multiple_of(i * block * docs, block * docs)
        scores = lax.dot_general(
            left[pl.ds(start, block * docs), :],
            right[...],
            (((1,), (1,)), ((), ())),
            preferred_element_type=jnp.float32,
        )
        for k in range(block):
            slot = 2 * (i * block + k)
            rows = scores[k * docs : (k + 1) * docs]
            best = jnp.maximum(best, jnp.where(counts > slot, rows[:, :query_rows], NOTHING))
            best = jnp.maximum(best, jnp.where(counts > slot + 1, rows[:, query_rows:], NOTHING))
        return best

    best = jnp.full((docs, query_rows), NOTHING, jnp.float32)
    if block == pairs:
        out_ref[...] = score(0, best)
    else:
        out_ref[...] = lax.fori_loop(0, pairs // block, score, best)


def local_maxima(left, live, spread, pieces, sources):
    docs = live.shape[0]
    query_rows = sum(piece.shape[0] for piece in pieces)
    return pl.pallas_call(
        functools.partial(score_kernel, sources, docs),
        out_shape=jax.ShapeDtypeStruct((docs, query_rows), jnp.float32),
        in_specs=[vmem()] * (3 + len(pieces)),
        out_specs=vmem(),
        scratch_shapes=[
            pltpu.VMEM((query_rows, DIM), jnp.float32),
            pltpu.VMEM((2 * query_rows, 4 * DIM), jnp.bfloat16),
        ],
        compiler_params=pltpu.CompilerParams(vmem_limit_bytes=24 * 2**20),
        name="local_maxima",
    )(left, live, spread, *pieces)


def rms_scale(values, gain):
    mean_square = jnp.mean(values * values, axis=-1, keepdims=True)
    return (values * lax.rsqrt(mean_square + 1e-06) * gain).astype(jnp.bfloat16)


def product(left, right):
    return jnp.dot(left, right, preferred_element_type=jnp.float32)


def rerank_kernel(sources, *refs):
    pieces, refs = refs[: len(sources)], refs[len(sources) :]
    (
        chosen,
        proj_parts,
        gain_one,
        query_proj,
        key_proj,
        value_proj,
        output_proj,
        gain_two,
        up_proj,
        down_proj,
        out_ref,
        maxima,
    ) = refs
    rows = out_ref.shape[0]
    cand = chosen.shape[0] - rows
    place(pieces, sources, maxima, "docs")

    width = maxima.shape[1]
    own = pltpu.roll(maxima[...], lax.rem(width - lax.axis_index("docs") * QT, width), 1)
    parts = three_parts(own[:, :QT])
    stacked = jnp.concatenate([parts[k[0]] for k in PART_PAIRS], axis=1)
    features = product(chosen[...], stacked).astype(jnp.bfloat16)
    all_hidden = product(features, proj_parts[...])
    hidden_zero = all_hidden[cand:]
    normed = rms_scale(all_hidden, gain_one[...])
    query_heads = product(normed[cand:], query_proj[...]).astype(jnp.bfloat16)
    key_heads = product(normed[:cand], key_proj[...]).astype(jnp.bfloat16)
    value_heads = product(normed[:cand], value_proj[...]).astype(jnp.bfloat16)

    head_of = jnp.right_shift(lax.broadcasted_iota(jnp.int32, (rows, H), 1), 6)
    split = [jnp.where(head_of == h, query_heads, jnp.zeros_like(query_heads)) for h in range(HEADS)]
    scores = lax.dot_general(
        jnp.concatenate(split, axis=0),
        key_heads,
        (((1,), (1,)), ((), ())),
        preferred_element_type=jnp.float32,
    ) * (HEAD ** (-0.5))
    expon = jnp.exp(scores - jnp.max(scores, axis=-1, keepdims=True))
    summed = jnp.sum(expon, axis=-1, keepdims=True)
    spread = product(expon.astype(jnp.bfloat16), value_heads) / summed
    attended = spread[:rows]
    for h in range(1, HEADS):
        attended = jnp.where(head_of == h, spread[h * rows : (h + 1) * rows], attended)
    hidden_one = hidden_zero + product(attended.astype(jnp.bfloat16), output_proj[...])
    normed_two = rms_scale(hidden_one, gain_two[...])
    inner = jax.nn.gelu(product(normed_two, up_proj[...])).astype(jnp.bfloat16)
    out_ref[...] = hidden_one + product(inner, down_proj[...])


def rerank(pieces, sources, arrays, rows):
    docs_all = sum(piece.shape[0] for piece in pieces)
    query_rows = pieces[0].shape[1]
    return pl.pallas_call(
        functools.partial(rerank_kernel, sources),
        out_shape=jax.ShapeDtypeStruct((rows, H), jnp.float32),
        in_specs=[vmem()] * (len(pieces) + len(arrays)),
        out_specs=vmem(),
        scratch_shapes=[pltpu.VMEM((docs_all, query_rows), jnp.float32)],
        compiler_params=pltpu.CompilerParams(vmem_limit_bytes=32 * 2**20),
        name="rerank",
    )(*pieces, *arrays)


def on_device(
    queries,
    token_codes,
    centroid_ids,
    slot_counts,
    centroids,
    bucket_values,
    candidates,
    input_proj,
    gain_one,
    query_proj,
    key_proj,
    value_proj,
    output_proj,
    gain_two,
    up_proj,
    down_proj,
):
    kept = (
        gain_one[None, :],
        query_proj,
        key_proj,
        value_proj,
        output_proj,
        gain_two[None, :],
        up_proj,
        down_proj,
    )
    docs_all = slot_counts.shape[1] * lax.axis_size("docs")
    rows = candidates.shape[1] // lax.axis_size(MEMBERS)
    query_pieces, query_sources = gather_queries(queries)
    left, live, spread, *staged = prepare(
        centroid_ids,
        slot_counts,
        candidates,
        token_codes[0],
        centroids,
        bucket_values,
        input_proj,
        docs_all,
        rows,
        kept,
    )
    local_best = local_maxima(left, live, spread, query_pieces, query_sources)
    doc_pieces, doc_sources = gather_docs(best_of_members(local_best))
    return rerank(doc_pieces, doc_sources, staged, rows)[None]


def solution(mesh):
    in_specs = (
        P(("groups", "cent", "sub"), None),
        P(("cent", "sub"), ("groups", "docs"), None),
        P(("cent", "sub"), ("groups", "docs")),
        P(("cent", "sub"), ("groups", "docs")),
        P(("cent", "sub"), None),
        P(),
        P(("groups", "docs"), None),
        P(),
        P(),
        P(),
        P(),
        P(),
        P(),
        P(),
        P(),
        P(),
    )
    out_specs = P(("groups", "docs"), ("cent", "sub"), None)
    return jax.shard_map(
        on_device, mesh=mesh, in_specs=in_specs, out_specs=out_specs, check_vma=False
    )
```

```python
import functools

import jax
import jax.numpy as jnp
from jax import lax
from jax.experimental import pallas as pl
from jax.experimental.pallas import tpu as pltpu
from jax.sharding import PartitionSpec as P

DIM = 128
QT = 32
H = 256
HEADS = 4
HEAD = 64
MEMBERS = ("cent", "sub")
NOTHING = -1e30
CHUNKS = 4
PART_PAIRS = ((0, 0), (0, 1), (0, 2), (1, 0), (1, 1), (2, 0))
FIRST_STEP = ((2, 3, 0, 1), (1, 2, 3, 0))
SECOND_STEP = (3, 0, 1, 2)


def compact():
    return (
        lax.axis_size("cent") == 2
        and lax.axis_size("sub") == 2
        and lax.axis_size("docs") == len(SECOND_STEP)
    )


def gather_queries(queries):
    if not compact():
        return [lax.all_gather(queries, MEMBERS, axis=0, tiled=True)], [None]
    pieces, sources = [queries], [[0, 1, 2, 3]]
    for step in (1, 2, 3):
        sources.append([i ^ step for i in range(4)])
        pieces.append(lax.ppermute(queries, MEMBERS, [(i, i ^ step) for i in range(4)]))
    return pieces, sources


def best_of_members(values):
    if not compact():
        return lax.pmax(values, MEMBERS)
    values = jnp.maximum(values, lax.ppermute(values, "sub", [(0, 1), (1, 0)]))
    return jnp.maximum(values, lax.ppermute(values, MEMBERS, [(i, i ^ 3) for i in range(4)]))


def gather_docs(values):
    if not compact():
        return [lax.all_gather(values, "docs", axis=0, tiled=True)], [None]
    axes = ("docs", "sub")
    places = [(d, c) for d in range(4) for c in range(2)]
    first = lax.ppermute(values, axes, [(2 * d + c, 2 * FIRST_STEP[c][d] + c) for d, c in places])
    second = lax.ppermute(
        values, axes, [(2 * d + c, 2 * SECOND_STEP[d] + 1 - c) for d, c in places]
    )
    other = lax.ppermute(first, "sub", [(0, 1), (1, 0)])
    sources = [
        [d for d, _ in places],
        [FIRST_STEP[c].index(d) for d, c in places],
        [FIRST_STEP[1 - c].index(d) for d, c in places],
        [SECOND_STEP.index(d) for d, _ in places],
    ]
    return [values, first, other, second], sources


def place(pieces, sources, out_ref, axes):
    if len(pieces) == 1:
        out_ref[...] = pieces[0][...]
        return
    me = lax.axis_index(axes)
    for piece, source in zip(pieces, sources):
        rows = piece.shape[0]
        place_of = jnp.int32(source[0])
        for i in range(1, len(source)):
            place_of = jnp.where(me == i, source[i], place_of)
        start = pl.multiple_of(place_of * rows, rows)
        out_ref[pl.ds(start, rows), :] = piece[...]


def vmem():
    return pl.BlockSpec(memory_space=pltpu.VMEM)


def smem():
    return pl.BlockSpec(memory_space=pltpu.SMEM)


def hbm():
    return pl.BlockSpec(memory_space=pltpu.HBM)


def in_hbm(array):
    return pltpu.with_memory_space_constraint(array, pltpu.HBM)


def even_odd_columns():
    wide = lax.broadcasted_iota(jnp.int32, (DIM, 2 * DIM), 1)
    dim = lax.broadcasted_iota(jnp.int32, (DIM, 2 * DIM), 0)
    wanted = 2 * jnp.bitwise_and(wide, 63) + jnp.right_shift(wide, 7)
    return jnp.where(wanted == dim, 1.0, 0.0).astype(jnp.bfloat16)


def three_parts(values):
    parts = []
    for _ in range(3):
        part = values.astype(jnp.bfloat16)
        values = values - part.astype(jnp.float32)
        parts.append(part)
    return parts


def look_up(nibbles, halves):
    index = jnp.bitwise_and(nibbles, 7)
    lower = jnp.take_along_axis(halves[0], index, axis=0)
    upper = jnp.take_along_axis(halves[1], index, axis=0)
    return jnp.where(nibbles >= 8, upper, lower)


def prepare_kernel(n_kept, *refs):
    ids_hbm, counts_hbm, candidates_hbm, codes_hbm, centroids_hbm, buckets_hbm, proj_hbm = refs[:7]
    kept_hbm, refs = refs[7 : 7 + n_kept], refs[7 + n_kept :]
    left, live, spread, chosen, proj_parts = refs[:5]
    kept, refs = refs[5 : 5 + n_kept], refs[5 + n_kept :]
    ids, counts, candidates, codes, centroids, buckets, proj, table, sems, chunk_sems, code_sems, kept_sems = refs
    docs, columns = codes.shape
    pairs = columns // DIM
    slots = 2 * pairs
    cand = candidates.shape[1]
    rows_dev = chosen.shape[0] - cand

    chunk = centroids.shape[0] // CHUNKS
    chunks = [
        pltpu.make_async_copy(
            centroids_hbm.at[pl.ds(i * chunk, chunk), :],
            centroids.at[pl.ds(i * chunk, chunk), :],
            chunk_sems.at[i],
        )
        for i in range(CHUNKS)
    ]
    small = [
        pltpu.make_async_copy(source, target, sems.at[i])
        for i, (source, target) in enumerate(
            (
                (ids_hbm, ids),
                (buckets_hbm, buckets),
                (counts_hbm, counts),
                (candidates_hbm, candidates),
                (proj_hbm, proj),
            )
        )
    ]
    part = columns // CHUNKS
    code_chunks = [
        pltpu.make_async_copy(
            codes_hbm.at[:, pl.ds(i * part, part)],
            codes.at[:, pl.ds(i * part, part)],
            code_sems.at[i],
        )
        for i in range(CHUNKS)
    ]
    late = [
        pltpu.make_async_copy(source, target, kept_sems.at[i])
        for i, (source, target) in enumerate(zip(kept_hbm, kept))
    ]
    for copy in small + chunks + code_chunks:
        copy.start()
    columns_of = even_odd_columns()
    spread[...] = columns_of

    small[1].wait()
    levels = jnp.dot(
        buckets[...].astype(jnp.bfloat16), columns_of, preferred_element_type=jnp.float32
    )
    tables = [[levels[i : i + 8, k : k + DIM] for i in (0, 8)] for k in (0, DIM)]
    small[2].wait()
    doc_row = lax.broadcasted_iota(jnp.int32, (8, DIM), 0)
    for b in range(docs // 8):
        block = jnp.zeros((8, DIM), jnp.int32)
        for n in range(8):
            block = jnp.where(doc_row == n, counts[0, b * 8 + n], block)
        live[b * 8 : b * 8 + 8, :] = block

    small[3].wait()
    docs_all = chosen.shape[1]
    member = lax.axis_index(MEMBERS)
    doc = lax.broadcasted_iota(jnp.int32, (16, docs_all), 1)
    place_in = lax.broadcasted_iota(jnp.int32, (16, docs_all), 0)

    def choose(i, carry):
        start = pl.multiple_of(i * 16, 16)
        source = jnp.where(start < cand, start, start - cand + member * rows_dev)
        wanted = jnp.zeros((16, docs_all), jnp.int32)
        for n in range(16):
            wanted = jnp.where(place_in == n, candidates[0, source + n], wanted)
        chosen[pl.ds(start, 16), :] = jnp.where(doc == wanted, 1.0, 0.0).astype(jnp.bfloat16)
        return carry

    lax.fori_loop(0, chosen.shape[0] // 16, choose, 0)
    small[4].wait()
    parts = three_parts(proj[...])
    for i, k in enumerate(PART_PAIRS):
        proj_parts[i * QT : (i + 1) * QT, :] = parts[k[1]]

    for i, copy in enumerate(chunks):
        copy.wait()
        for first in range(i * chunk, (i + 1) * chunk, 256):
            table[first : first + 256, :] = centroids[first : first + 256, :].astype(jnp.float32)
    small[0].wait()
    row_bits = [jnp.bitwise_and(doc_row, bit) != 0 for bit in (1, 2, 4)]

    def fetch(slot, first):
        rows = []
        for n in range(first, first + 8):
            row = table[pl.ds(ids[0, n * slots + slot], 1), :]
            rows.append(jnp.broadcast_to(row, (8, DIM)))
        for bit in row_bits:
            rows = [jnp.where(bit, rows[i + 1], rows[i]) for i in range(0, len(rows), 2)]
        return rows[0]

    def one_pair(pair, carry):
        start = pl.multiple_of(pair * docs, docs)
        column = pl.multiple_of(pair * DIM, DIM)
        parts = [[], [], [], []]
        for b in range(0, docs, 8):
            code = codes[b : b + 8, pl.ds(column, DIM)]
            parts[0].append(fetch(2 * pair, b))
            parts[1].append(fetch(2 * pair + 1, b))
            parts[2].append(look_up(jnp.bitwise_and(code, 15), tables[0]))
            parts[3].append(look_up(jnp.right_shift(code, 4), tables[1]))
        for k, part in enumerate(parts):
            columns = slice(k * DIM, (k + 1) * DIM)
            left[pl.ds(start, docs), columns] = jnp.concatenate(part, axis=0).astype(jnp.bfloat16)
        return carry

    for i, copy in enumerate(code_chunks):
        copy.wait()
        if i == 1:
            for other in late:
                other.start()
        lax.fori_loop(
            i * pairs // CHUNKS, (i + 1) * pairs // CHUNKS, one_pair, 0, unroll=True
        )
    for copy in late:
        copy.wait()


def prepare(ids, counts, candidates, codes, centroids, buckets, input_proj, docs_all, rows, kept):
    docs, columns = codes.shape
    pairs = columns // DIM
    shape = jax.ShapeDtypeStruct
    return pl.pallas_call(
        functools.partial(prepare_kernel, len(kept)),
        out_shape=[
            shape((pairs * docs, 4 * DIM), jnp.bfloat16),
            shape((docs, DIM), jnp.int32),
            shape((DIM, 2 * DIM), jnp.bfloat16),
            shape((candidates.shape[1] + rows, docs_all), jnp.bfloat16),
            shape((len(PART_PAIRS) * QT, H), jnp.bfloat16),
        ]
        + [shape(array.shape, array.dtype) for array in kept],
        in_specs=[hbm()] * (7 + len(kept)),
        out_specs=[vmem()] * (5 + len(kept)),
        scratch_shapes=[
            pltpu.SMEM(ids.shape, jnp.int32),
            pltpu.SMEM(counts.shape, jnp.int32),
            pltpu.SMEM(candidates.shape, jnp.int32),
            pltpu.VMEM(codes.shape, jnp.int32),
            pltpu.VMEM(centroids.shape, jnp.bfloat16),
            pltpu.VMEM(buckets.shape, jnp.float32),
            pltpu.VMEM(input_proj.shape, jnp.float32),
            pltpu.VMEM(centroids.shape, jnp.float32),
            pltpu.SemaphoreType.DMA((5,)),
            pltpu.SemaphoreType.DMA((CHUNKS,)),
            pltpu.SemaphoreType.DMA((CHUNKS,)),
            pltpu.SemaphoreType.DMA((len(kept),)),
        ],
        compiler_params=pltpu.CompilerParams(vmem_limit_bytes=24 * 2**20),
        cost_estimate=pl.CostEstimate(flops=4 * 10**9, bytes_accessed=2**22, transcendentals=0),
        name="prepare",
    )(
        *[
            in_hbm(x)
            for x in (ids, counts, candidates, codes, centroids, buckets, input_proj, *kept)
        ]
    )


def score_kernel(sources, docs, left, live, spread, *refs):
    pieces, (out_ref, queries, right) = refs[: len(sources)], refs[len(sources) :]
    query_rows = queries.shape[0]
    pairs = left.shape[0] // docs
    place(pieces, sources, queries, MEMBERS)
    query_bf = queries[...].astype(jnp.bfloat16)
    query_pair = jnp.dot(query_bf, spread[...], preferred_element_type=jnp.float32)
    lane = lax.broadcasted_iota(jnp.int32, (query_rows, 2 * DIM), 1)
    first = jnp.bitwise_and(lane, 64) == 0
    none = jnp.zeros((query_rows, DIM), jnp.bfloat16)
    right[:query_rows, :DIM] = query_bf
    right[:query_rows, DIM : 2 * DIM] = none
    right[:query_rows, 2 * DIM :] = jnp.where(first, query_pair, 0.0).astype(jnp.bfloat16)
    right[query_rows:, :DIM] = none
    right[query_rows:, DIM : 2 * DIM] = query_bf
    right[query_rows:, 2 * DIM :] = jnp.where(first, 0.0, query_pair).astype(jnp.bfloat16)

    counts = jnp.concatenate([live[...]] * (query_rows // DIM), axis=1)
    block = pairs if query_rows == DIM else 4

    def score(i, best):
        start = pl.multiple_of(i * block * docs, block * docs)
        scores = lax.dot_general(
            left[pl.ds(start, block * docs), :],
            right[...],
            (((1,), (1,)), ((), ())),
            preferred_element_type=jnp.float32,
        )
        for k in range(block):
            slot = 2 * (i * block + k)
            rows = scores[k * docs : (k + 1) * docs]
            best = jnp.maximum(best, jnp.where(counts > slot, rows[:, :query_rows], NOTHING))
            best = jnp.maximum(best, jnp.where(counts > slot + 1, rows[:, query_rows:], NOTHING))
        return best

    best = jnp.full((docs, query_rows), NOTHING, jnp.float32)
    if block == pairs:
        out_ref[...] = score(0, best)
    else:
        out_ref[...] = lax.fori_loop(0, pairs // block, score, best)


def local_maxima(left, live, spread, pieces, sources):
    docs = live.shape[0]
    query_rows = sum(piece.shape[0] for piece in pieces)
    return pl.pallas_call(
        functools.partial(score_kernel, sources, docs),
        out_shape=jax.ShapeDtypeStruct((docs, query_rows), jnp.float32),
        in_specs=[vmem()] * (3 + len(pieces)),
        out_specs=vmem(),
        scratch_shapes=[
            pltpu.VMEM((query_rows, DIM), jnp.float32),
            pltpu.VMEM((2 * query_rows, 4 * DIM), jnp.bfloat16),
        ],
        compiler_params=pltpu.CompilerParams(vmem_limit_bytes=24 * 2**20),
        name="local_maxima",
    )(left, live, spread, *pieces)


def rms_scale(values, gain):
    mean_square = jnp.mean(values * values, axis=-1, keepdims=True)
    return (values * lax.rsqrt(mean_square + 1e-06) * gain).astype(jnp.bfloat16)


def product(left, right):
    return jnp.dot(left, right, preferred_element_type=jnp.float32)


def rerank_kernel(sources, *refs):
    pieces, refs = refs[: len(sources)], refs[len(sources) :]
    (
        chosen,
        proj_parts,
        gain_one,
        query_proj,
        key_proj,
        value_proj,
        output_proj,
        gain_two,
        up_proj,
        down_proj,
        out_ref,
        maxima,
    ) = refs
    rows = out_ref.shape[0]
    cand = chosen.shape[0] - rows
    place(pieces, sources, maxima, ("docs", "sub"))

    width = maxima.shape[1]
    own = pltpu.roll(maxima[...], lax.rem(width - lax.axis_index("docs") * QT, width), 1)
    parts = three_parts(own[:, :QT])
    stacked = jnp.concatenate([parts[k[0]] for k in PART_PAIRS], axis=1)
    features = product(chosen[...], stacked).astype(jnp.bfloat16)
    all_hidden = product(features, proj_parts[...])
    hidden_zero = all_hidden[cand:]
    normed = rms_scale(all_hidden, gain_one[...])
    query_heads = product(normed[cand:], query_proj[...]).astype(jnp.bfloat16)
    key_heads = product(normed[:cand], key_proj[...]).astype(jnp.bfloat16)
    value_heads = product(normed[:cand], value_proj[...]).astype(jnp.bfloat16)

    head_of = jnp.right_shift(lax.broadcasted_iota(jnp.int32, (rows, H), 1), 6)
    split = [jnp.where(head_of == h, query_heads, jnp.zeros_like(query_heads)) for h in range(HEADS)]
    scores = lax.dot_general(
        jnp.concatenate(split, axis=0),
        key_heads,
        (((1,), (1,)), ((), ())),
        preferred_element_type=jnp.float32,
    ) * (HEAD ** (-0.5))
    expon = jnp.exp(scores - jnp.max(scores, axis=-1, keepdims=True))
    summed = jnp.sum(expon, axis=-1, keepdims=True)
    spread = product(expon.astype(jnp.bfloat16), value_heads) / summed
    attended = spread[:rows]
    for h in range(1, HEADS):
        attended = jnp.where(head_of == h, spread[h * rows : (h + 1) * rows], attended)
    hidden_one = hidden_zero + product(attended.astype(jnp.bfloat16), output_proj[...])
    normed_two = rms_scale(hidden_one, gain_two[...])
    inner = jax.nn.gelu(product(normed_two, up_proj[...])).astype(jnp.bfloat16)
    out_ref[...] = hidden_one + product(inner, down_proj[...])


def rerank(pieces, sources, arrays, rows):
    docs_all = sum(piece.shape[0] for piece in pieces)
    query_rows = pieces[0].shape[1]
    return pl.pallas_call(
        functools.partial(rerank_kernel, sources),
        out_shape=jax.ShapeDtypeStruct((rows, H), jnp.float32),
        in_specs=[vmem()] * (len(pieces) + len(arrays)),
        out_specs=vmem(),
        scratch_shapes=[pltpu.VMEM((docs_all, query_rows), jnp.float32)],
        compiler_params=pltpu.CompilerParams(vmem_limit_bytes=32 * 2**20),
        name="rerank",
    )(*pieces, *arrays)


def on_device(
    queries,
    token_codes,
    centroid_ids,
    slot_counts,
    centroids,
    bucket_values,
    candidates,
    input_proj,
    gain_one,
    query_proj,
    key_proj,
    value_proj,
    output_proj,
    gain_two,
    up_proj,
    down_proj,
):
    kept = (
        gain_one[None, :],
        query_proj,
        key_proj,
        value_proj,
        output_proj,
        gain_two[None, :],
        up_proj,
        down_proj,
    )
    docs_all = slot_counts.shape[1] * lax.axis_size("docs")
    rows = candidates.shape[1] // lax.axis_size(MEMBERS)
    query_pieces, query_sources = gather_queries(queries)
    left, live, spread, *staged = prepare(
        centroid_ids,
        slot_counts,
        candidates,
        token_codes[0],
        centroids,
        bucket_values,
        input_proj,
        docs_all,
        rows,
        kept,
    )
    local_best = local_maxima(left, live, spread, query_pieces, query_sources)
    doc_pieces, doc_sources = gather_docs(best_of_members(local_best))
    return rerank(doc_pieces, doc_sources, staged, rows)[None]


def solution(mesh):
    in_specs = (
        P(("groups", "cent", "sub"), None),
        P(("cent", "sub"), ("groups", "docs"), None),
        P(("cent", "sub"), ("groups", "docs")),
        P(("cent", "sub"), ("groups", "docs")),
        P(("cent", "sub"), None),
        P(),
        P(("groups", "docs"), None),
        P(),
        P(),
        P(),
        P(),
        P(),
        P(),
        P(),
        P(),
        P(),
    )
    out_specs = P(("groups", "docs"), ("cent", "sub"), None)
    return jax.shard_map(
        on_device, mesh=mesh, in_specs=in_specs, out_specs=out_specs, check_vma=False
    )
```

```python
import functools

import jax
import jax.numpy as jnp
from jax import lax
from jax.experimental import pallas as pl
from jax.experimental.pallas import tpu as pltpu
from jax.sharding import PartitionSpec as P

DIM = 128
QT = 32
H = 256
HEADS = 4
HEAD = 64
MEMBERS = ("cent", "sub")
NOTHING = -1e30
PART_PAIRS = ((0, 0), (0, 1), (0, 2), (1, 0), (1, 1), (2, 0))
QUERY_STEPS = ((2, 3, 1, 0), (1, 0, 3, 2), (3, 2, 0, 1))
FIRST_STEP = ((2, 3, 0, 1), (1, 2, 3, 0))
SECOND_STEP = (3, 0, 1, 2)


def compact():
    return (
        lax.axis_size("cent") == 2
        and lax.axis_size("sub") == 2
        and lax.axis_size("docs") == len(SECOND_STEP)
    )


def gather_queries(queries):
    if not compact():
        return [lax.all_gather(queries, MEMBERS, axis=0, tiled=True)], [None]
    pieces, sources = [queries], [[0, 1, 2, 3]]
    for step in QUERY_STEPS:
        sources.append([step.index(i) for i in range(4)])
        pieces.append(lax.ppermute(queries, MEMBERS, list(enumerate(step))))
    return pieces, sources


def best_of_members(values):
    if not compact():
        return lax.pmax(values, MEMBERS)
    values = jnp.maximum(values, lax.ppermute(values, "sub", [(0, 1), (1, 0)]))
    return jnp.maximum(values, lax.ppermute(values, MEMBERS, [(i, i ^ 3) for i in range(4)]))


def gather_docs(values):
    if not compact():
        return [lax.all_gather(values, "docs", axis=0, tiled=True)], [None]
    axes = ("docs", "sub")
    places = [(d, c) for d in range(4) for c in range(2)]
    first = lax.ppermute(values, axes, [(2 * d + c, 2 * FIRST_STEP[c][d] + c) for d, c in places])
    second = lax.ppermute(
        values, axes, [(2 * d + c, 2 * SECOND_STEP[d] + 1 - c) for d, c in places]
    )
    other = lax.ppermute(first, "sub", [(0, 1), (1, 0)])
    sources = [
        [d for d, _ in places],
        [FIRST_STEP[c].index(d) for d, c in places],
        [FIRST_STEP[1 - c].index(d) for d, c in places],
        [SECOND_STEP.index(d) for d, _ in places],
    ]
    return [values, first, other, second], sources


def place(pieces, sources, out_ref, axes):
    if len(pieces) == 1:
        out_ref[...] = pieces[0][...]
        return
    me = lax.axis_index(axes)
    for piece, source in zip(pieces, sources):
        rows = piece.shape[0]
        place_of = jnp.int32(source[0])
        for i in range(1, len(source)):
            place_of = jnp.where(me == i, source[i], place_of)
        start = pl.multiple_of(place_of * rows, rows)
        out_ref[pl.ds(start, rows), :] = piece[...]


def vmem():
    return pl.BlockSpec(memory_space=pltpu.VMEM)


def smem():
    return pl.BlockSpec(memory_space=pltpu.SMEM)


def hbm():
    return pl.BlockSpec(memory_space=pltpu.HBM)


def in_hbm(array):
    return pltpu.with_memory_space_constraint(array, pltpu.HBM)


def even_odd_columns():
    column = lax.broadcasted_iota(jnp.int32, (DIM, DIM), 1)
    dim = lax.broadcasted_iota(jnp.int32, (DIM, DIM), 0)
    wanted = 2 * jnp.bitwise_and(column, 63) + jnp.right_shift(column, 6)
    return jnp.where(wanted == dim, 1.0, 0.0).astype(jnp.bfloat16)


def product(left, right):
    return jnp.dot(left, right, preferred_element_type=jnp.float32)


def three_parts(values):
    parts = []
    for _ in range(3):
        part = values.astype(jnp.bfloat16)
        values = values - part.astype(jnp.float32)
        parts.append(part)
    return parts


def look_up(nibbles, halves):
    index = jnp.bitwise_and(nibbles, 7)
    lower = jnp.take_along_axis(halves[0], index, axis=0)
    upper = jnp.take_along_axis(halves[1], index, axis=0)
    return jnp.where(nibbles >= 8, upper, lower)


def early_kernel(spread):
    spread[...] = even_odd_columns()


def early():
    return pl.pallas_call(
        early_kernel,
        out_shape=jax.ShapeDtypeStruct((DIM, DIM), jnp.bfloat16),
        out_specs=vmem(),
        compiler_params=pltpu.CompilerParams(vmem_limit_bytes=4 * 2**20),
        cost_estimate=pl.CostEstimate(flops=4 * 10**9, bytes_accessed=0, transcendentals=0),
        name="early",
    )()


def prepare_kernel(n_kept, ids_vmem, codes, centroids, buckets, spread, counts_hbm, *refs):
    kept_hbm, (left, live), refs = refs[:n_kept], refs[n_kept : n_kept + 2], refs[n_kept + 2 :]
    kept, (ids, counts, table, sems, kept_sems) = refs[:n_kept], refs[n_kept:]
    docs, columns = codes.shape
    pairs = columns // DIM
    slots = 2 * pairs
    scalars = [
        pltpu.make_async_copy(source, target, sems.at[i])
        for i, (source, target) in enumerate(((ids_vmem, ids), (counts_hbm, counts)))
    ]
    late = [
        pltpu.make_async_copy(source, target, kept_sems.at[i])
        for i, (source, target) in enumerate(zip(kept_hbm, kept))
    ]
    for copy in scalars + late:
        copy.start()
    levels = sum(product(part, spread[...]) for part in three_parts(buckets[...]))
    halves = [levels[:8], levels[8:]]
    for first in range(0, centroids.shape[0], 512):
        table[first : first + 512, :] = product(centroids[first : first + 512, :], spread[...])
    first_half = lax.broadcasted_iota(jnp.int32, (8, DIM), 1) < DIM // 2
    doc_row = lax.broadcasted_iota(jnp.int32, (8, DIM), 0)
    scalars[0].wait()
    row_bits = [jnp.bitwise_and(doc_row, bit) != 0 for bit in (1, 2, 4)]

    def fetch(slot, first):
        rows = []
        for n in range(first, first + 8):
            row = table[pl.ds(ids[0, n * slots + slot], 1), :]
            rows.append(jnp.broadcast_to(row, (8, DIM)))
        for bit in row_bits:
            rows = [jnp.where(bit, rows[i + 1], rows[i]) for i in range(0, len(rows), 2)]
        return rows[0]

    def one_pair(pair, carry):
        start = pl.multiple_of(pair * docs, docs)
        column = pl.multiple_of(pair * DIM, DIM)
        parts = [[], []]
        for b in range(0, docs, 8):
            code = codes[b : b + 8, pl.ds(column, DIM)]
            other = pltpu.roll(code, DIM // 2, 1)
            nibbles = (
                jnp.where(first_half, jnp.bitwise_and(code, 15), jnp.right_shift(other, 4)),
                jnp.where(first_half, jnp.bitwise_and(other, 15), jnp.right_shift(code, 4)),
            )
            for k in range(2):
                parts[k].append(fetch(2 * pair + k, b) + look_up(nibbles[k], halves))
        for k, part in enumerate(parts):
            columns = slice(k * DIM, (k + 1) * DIM)
            left[pl.ds(start, docs), columns] = jnp.concatenate(part, axis=0).astype(jnp.bfloat16)
        return carry

    lax.fori_loop(0, pairs, one_pair, 0, unroll=True)
    scalars[1].wait()
    for b in range(docs // 8):
        block = jnp.zeros((8, DIM), jnp.int32)
        for n in range(8):
            block = jnp.where(doc_row == n, counts[0, b * 8 + n], block)
        live[b * 8 : b * 8 + 8, :] = block
    for copy in late:
        copy.wait()


def prepare(ids, counts, codes, centroids, buckets, spread, kept):
    docs, columns = codes.shape
    pairs = columns // DIM
    shape = jax.ShapeDtypeStruct
    return pl.pallas_call(
        functools.partial(prepare_kernel, len(kept)),
        out_shape=[
            shape((pairs * docs, 2 * DIM), jnp.bfloat16),
            shape((docs, DIM), jnp.int32),
        ]
        + [shape(array.shape, array.dtype) for array in kept],
        in_specs=[vmem()] * 5 + [hbm()] * (1 + len(kept)),
        out_specs=[vmem()] * (2 + len(kept)),
        scratch_shapes=[
            pltpu.SMEM(ids.shape, jnp.int32),
            pltpu.SMEM(counts.shape, jnp.int32),
            pltpu.VMEM(centroids.shape, jnp.float32),
            pltpu.SemaphoreType.DMA((2,)),
            pltpu.SemaphoreType.DMA((len(kept),)),
        ],
        compiler_params=pltpu.CompilerParams(vmem_limit_bytes=24 * 2**20),
        cost_estimate=pl.CostEstimate(flops=4 * 10**9, bytes_accessed=2**22, transcendentals=0),
        name="prepare",
    )(ids, codes, centroids, buckets, spread, *[in_hbm(x) for x in (counts, *kept)])


def tables_kernel(candidates_vmem, proj, _, chosen, proj_parts, candidates, sem):
    cand = candidates.shape[1]
    rows_dev = chosen.shape[0] - cand
    copy = pltpu.make_async_copy(candidates_vmem, candidates, sem)
    copy.start()
    parts = three_parts(proj[...])
    for i, k in enumerate(PART_PAIRS):
        proj_parts[i * QT : (i + 1) * QT, :] = parts[k[1]]

    copy.wait()
    docs_all = chosen.shape[1]
    member = lax.axis_index(MEMBERS)
    doc = lax.broadcasted_iota(jnp.int32, (16, docs_all), 1)
    place_in = lax.broadcasted_iota(jnp.int32, (16, docs_all), 0)

    def choose(i, carry):
        start = pl.multiple_of(i * 16, 16)
        source = jnp.where(start < cand, start, start - cand + member * rows_dev)
        wanted = jnp.zeros((16, docs_all), jnp.int32)
        for n in range(16):
            wanted = jnp.where(place_in == n, candidates[0, source + n], wanted)
        chosen[pl.ds(start, 16), :] = jnp.where(doc == wanted, 1.0, 0.0).astype(jnp.bfloat16)
        return carry

    lax.fori_loop(0, chosen.shape[0] // 16, choose, 0)


def make_tables(candidates, input_proj, best, docs_all, rows):
    shape = jax.ShapeDtypeStruct
    return pl.pallas_call(
        tables_kernel,
        out_shape=[
            shape((candidates.shape[1] + rows, docs_all), jnp.bfloat16),
            shape((len(PART_PAIRS) * QT, H), jnp.bfloat16),
        ],
        in_specs=[vmem(), vmem(), pl.BlockSpec(memory_space=pl.ANY)],
        out_specs=[vmem()] * 2,
        scratch_shapes=[pltpu.SMEM(candidates.shape, jnp.int32), pltpu.SemaphoreType.DMA],
        compiler_params=pltpu.CompilerParams(vmem_limit_bytes=16 * 2**20),
        cost_estimate=pl.CostEstimate(flops=5 * 10**8, bytes_accessed=0, transcendentals=0),
        name="make_tables",
    )(candidates, input_proj, best)


def score_kernel(sources, docs, left, live, spread, *refs):
    pieces, (out_ref, queries, right) = refs[: len(sources)], refs[len(sources) :]
    query_rows = queries.shape[0]
    pairs = left.shape[0] // docs
    place(pieces, sources, queries, MEMBERS)
    query_bf = queries[...].astype(jnp.bfloat16)
    query_bf = product(query_bf, spread[...]).astype(jnp.bfloat16)
    none = jnp.zeros((query_rows, DIM), jnp.bfloat16)
    right[:query_rows, :DIM] = query_bf
    right[:query_rows, DIM:] = none
    right[query_rows:, :DIM] = none
    right[query_rows:, DIM:] = query_bf

    counts = jnp.concatenate([live[...]] * (query_rows // DIM), axis=1)
    block = pairs if query_rows == DIM else 4

    def score(i, best):
        start = pl.multiple_of(i * block * docs, block * docs)
        scores = lax.dot_general(
            left[pl.ds(start, block * docs), :],
            right[...],
            (((1,), (1,)), ((), ())),
            preferred_element_type=jnp.float32,
        )
        for k in range(block):
            slot = 2 * (i * block + k)
            rows = scores[k * docs : (k + 1) * docs]
            best = jnp.maximum(best, jnp.where(counts > slot, rows[:, :query_rows], NOTHING))
            best = jnp.maximum(best, jnp.where(counts > slot + 1, rows[:, query_rows:], NOTHING))
        return best

    best = jnp.full((docs, query_rows), NOTHING, jnp.float32)
    if block == pairs:
        out_ref[...] = score(0, best)
    else:
        out_ref[...] = lax.fori_loop(0, pairs // block, score, best)


def local_maxima(left, live, spread, pieces, sources):
    docs = live.shape[0]
    query_rows = sum(piece.shape[0] for piece in pieces)
    return pl.pallas_call(
        functools.partial(score_kernel, sources, docs),
        out_shape=jax.ShapeDtypeStruct((docs, query_rows), jnp.float32),
        in_specs=[vmem()] * (3 + len(pieces)),
        out_specs=vmem(),
        scratch_shapes=[
            pltpu.VMEM((query_rows, DIM), jnp.float32),
            pltpu.VMEM((2 * query_rows, 2 * DIM), jnp.bfloat16),
        ],
        compiler_params=pltpu.CompilerParams(vmem_limit_bytes=24 * 2**20),
        name="local_maxima",
    )(left, live, spread, *pieces)


def rms_scale(values, gain):
    mean_square = jnp.mean(values * values, axis=-1, keepdims=True)
    return (values * lax.rsqrt(mean_square + 1e-06) * gain).astype(jnp.bfloat16)


def rerank_kernel(sources, *refs):
    pieces, refs = refs[: len(sources)], refs[len(sources) :]
    (
        chosen,
        proj_parts,
        gain_one,
        query_proj,
        key_proj,
        value_proj,
        output_proj,
        gain_two,
        up_proj,
        down_proj,
        out_ref,
        maxima,
    ) = refs
    rows = out_ref.shape[0]
    cand = chosen.shape[0] - rows
    place(pieces, sources, maxima, ("docs", "sub"))

    width = maxima.shape[1]
    own = pltpu.roll(maxima[...], lax.rem(width - lax.axis_index("docs") * QT, width), 1)
    parts = three_parts(own[:, :QT])
    stacked = jnp.concatenate([parts[k[0]] for k in PART_PAIRS], axis=1)
    features = product(chosen[...], stacked).astype(jnp.bfloat16)
    all_hidden = product(features, proj_parts[...])
    hidden_zero = all_hidden[cand:]
    normed = rms_scale(all_hidden, gain_one[...])
    query_heads = product(normed[cand:], query_proj[...]).astype(jnp.bfloat16)
    key_heads = product(normed[:cand], key_proj[...]).astype(jnp.bfloat16)
    value_heads = product(normed[:cand], value_proj[...]).astype(jnp.bfloat16)

    head_of = jnp.right_shift(lax.broadcasted_iota(jnp.int32, (rows, H), 1), 6)
    split = [jnp.where(head_of == h, query_heads, jnp.zeros_like(query_heads)) for h in range(HEADS)]
    scores = lax.dot_general(
        jnp.concatenate(split, axis=0),
        key_heads,
        (((1,), (1,)), ((), ())),
        preferred_element_type=jnp.float32,
    ) * (HEAD ** (-0.5))
    expon = jnp.exp(scores - jnp.max(scores, axis=-1, keepdims=True))
    summed = jnp.sum(expon, axis=-1, keepdims=True)
    spread = product(expon.astype(jnp.bfloat16), value_heads) / summed
    attended = spread[:rows]
    for h in range(1, HEADS):
        attended = jnp.where(head_of == h, spread[h * rows : (h + 1) * rows], attended)
    hidden_one = hidden_zero + product(attended.astype(jnp.bfloat16), output_proj[...])
    normed_two = rms_scale(hidden_one, gain_two[...])
    inner = jax.nn.gelu(product(normed_two, up_proj[...])).astype(jnp.bfloat16)
    out_ref[...] = hidden_one + product(inner, down_proj[...])


def rerank(pieces, sources, arrays, rows):
    docs_all = sum(piece.shape[0] for piece in pieces)
    query_rows = pieces[0].shape[1]
    return pl.pallas_call(
        functools.partial(rerank_kernel, sources),
        out_shape=jax.ShapeDtypeStruct((rows, H), jnp.float32),
        in_specs=[vmem()] * (len(pieces) + len(arrays)),
        out_specs=vmem(),
        scratch_shapes=[pltpu.VMEM((docs_all, query_rows), jnp.float32)],
        compiler_params=pltpu.CompilerParams(vmem_limit_bytes=32 * 2**20),
        name="rerank",
    )(*pieces, *arrays)


def on_device(
    queries,
    token_codes,
    centroid_ids,
    slot_counts,
    centroids,
    bucket_values,
    candidates,
    input_proj,
    gain_one,
    query_proj,
    key_proj,
    value_proj,
    output_proj,
    gain_two,
    up_proj,
    down_proj,
):
    kept = (
        gain_one[None, :],
        query_proj,
        key_proj,
        value_proj,
        output_proj,
        gain_two[None, :],
        up_proj,
        down_proj,
    )
    docs_all = slot_counts.shape[1] * lax.axis_size("docs")
    rows = candidates.shape[1] // lax.axis_size(MEMBERS)
    query_pieces, query_sources = gather_queries(queries)
    spread = early()
    left, live, *staged = prepare(
        centroid_ids, slot_counts, token_codes[0], centroids, bucket_values, spread, kept
    )
    local_best = local_maxima(left, live, spread, query_pieces, query_sources)
    tables = make_tables(candidates, input_proj, local_best, docs_all, rows)
    doc_pieces, doc_sources = gather_docs(best_of_members(local_best))
    return rerank(doc_pieces, doc_sources, [*tables, *staged], rows)[None]


def solution(mesh):
    in_specs = (
        P(("groups", "cent", "sub"), None),
        P(("cent", "sub"), ("groups", "docs"), None),
        P(("cent", "sub"), ("groups", "docs")),
        P(("cent", "sub"), ("groups", "docs")),
        P(("cent", "sub"), None),
        P(),
        P(("groups", "docs"), None),
        P(),
        P(),
        P(),
        P(),
        P(),
        P(),
        P(),
        P(),
        P(),
    )
    out_specs = P(("groups", "docs"), ("cent", "sub"), None)
    return jax.shard_map(
        on_device, mesh=mesh, in_specs=in_specs, out_specs=out_specs, check_vma=False
    )
```

```python
import functools

import jax
import jax.numpy as jnp
from jax import lax
from jax.experimental import pallas as pl
from jax.experimental.pallas import tpu as pltpu
from jax.sharding import PartitionSpec as P

DIM = 128
QT = 32
H = 256
HEADS = 4
HEAD = 64
MEMBERS = ("cent", "sub")
NOTHING = -1e30
PART_PAIRS = ((0, 0), (0, 1), (0, 2), (1, 0), (1, 1), (2, 0))
QUERY_STEPS = ((2, 3, 1, 0), (1, 0, 3, 2), (3, 2, 0, 1))
FIRST_STEP = (4, 9, 11, 6, 8, 13, 10, 15, 12, 0, 2, 14, 5, 1, 7, 3)
SECOND_STEP = (13, 12, 15, 14, 0, 1, 3, 2, 5, 4, 6, 7, 10, 8, 11, 9)


def compact():
    return (
        lax.axis_size("cent") == 2
        and lax.axis_size("sub") == 2
        and 4 * lax.axis_size("docs") == len(SECOND_STEP)
    )


def gather_queries(queries):
    if not compact():
        return [lax.all_gather(queries, MEMBERS, axis=0, tiled=True)], [None]
    pieces, sources = [queries], [[0, 1, 2, 3]]
    for step in QUERY_STEPS:
        sources.append([step.index(i) for i in range(4)])
        pieces.append(lax.ppermute(queries, MEMBERS, list(enumerate(step))))
    return pieces, sources


def best_of_members(values):
    if not compact():
        return lax.pmax(values, MEMBERS)
    values = jnp.maximum(values, lax.ppermute(values, "sub", [(0, 1), (1, 0)]))
    return jnp.maximum(values, lax.ppermute(values, MEMBERS, [(i, i ^ 3) for i in range(4)]))


def gather_docs(values):
    if not compact():
        return [lax.all_gather(values, "docs", axis=0, tiled=True)], [None]
    axes = ("docs", "cent", "sub")
    first = lax.ppermute(values, axes, list(enumerate(FIRST_STEP)))
    second = lax.ppermute(values, axes, list(enumerate(SECOND_STEP)))
    other = lax.ppermute(first, "sub", [(0, 1), (1, 0)])
    places = range(len(FIRST_STEP))
    sources = [
        [i // 4 for i in places],
        [FIRST_STEP.index(i) // 4 for i in places],
        [FIRST_STEP.index(i ^ 1) // 4 for i in places],
        [SECOND_STEP.index(i) // 4 for i in places],
    ]
    return [values, first, other, second], sources


def place(pieces, sources, out_ref, axes):
    if len(pieces) == 1:
        out_ref[...] = pieces[0][...]
        return
    me = lax.axis_index(axes)
    for piece, source in zip(pieces, sources):
        rows = piece.shape[0]
        place_of = jnp.int32(source[0])
        for i in range(1, len(source)):
            place_of = jnp.where(me == i, source[i], place_of)
        start = pl.multiple_of(place_of * rows, rows)
        out_ref[pl.ds(start, rows), :] = piece[...]


def vmem():
    return pl.BlockSpec(memory_space=pltpu.VMEM)


def smem():
    return pl.BlockSpec(memory_space=pltpu.SMEM)


def hbm():
    return pl.BlockSpec(memory_space=pltpu.HBM)


def in_hbm(array):
    return pltpu.with_memory_space_constraint(array, pltpu.HBM)


def even_odd_columns():
    column = lax.broadcasted_iota(jnp.int32, (DIM, DIM), 1)
    dim = lax.broadcasted_iota(jnp.int32, (DIM, DIM), 0)
    wanted = 2 * jnp.bitwise_and(column, 63) + jnp.right_shift(column, 6)
    return jnp.where(wanted == dim, 1.0, 0.0).astype(jnp.bfloat16)


def product(left, right):
    return jnp.dot(left, right, preferred_element_type=jnp.float32)


def three_parts(values):
    parts = []
    for _ in range(3):
        part = values.astype(jnp.bfloat16)
        values = values - part.astype(jnp.float32)
        parts.append(part)
    return parts


def look_up(nibbles, halves):
    index = jnp.bitwise_and(nibbles, 7)
    lower = jnp.take_along_axis(halves[0], index, axis=0)
    upper = jnp.take_along_axis(halves[1], index, axis=0)
    return jnp.where(nibbles >= 8, upper, lower)


def early_kernel(spread):
    spread[...] = even_odd_columns()


def early():
    return pl.pallas_call(
        early_kernel,
        out_shape=jax.ShapeDtypeStruct((DIM, DIM), jnp.bfloat16),
        out_specs=vmem(),
        compiler_params=pltpu.CompilerParams(vmem_limit_bytes=4 * 2**20),
        cost_estimate=pl.CostEstimate(flops=4 * 10**9, bytes_accessed=0, transcendentals=0),
        name="early",
    )()


def prepare_kernel(n_kept, ids_vmem, codes, centroids, buckets, spread, counts_hbm, *refs):
    kept_hbm, (left, live), refs = refs[:n_kept], refs[n_kept : n_kept + 2], refs[n_kept + 2 :]
    kept, (ids, counts, table, sems, kept_sems) = refs[:n_kept], refs[n_kept:]
    docs, columns = codes.shape
    pairs = columns // DIM
    slots = 2 * pairs
    scalars = [
        pltpu.make_async_copy(source, target, sems.at[i])
        for i, (source, target) in enumerate(((ids_vmem, ids), (counts_hbm, counts)))
    ]
    late = [
        pltpu.make_async_copy(source, target, kept_sems.at[i])
        for i, (source, target) in enumerate(zip(kept_hbm, kept))
    ]
    for copy in scalars + late:
        copy.start()
    levels = sum(product(part, spread[...]) for part in three_parts(buckets[...]))
    halves = [levels[:8], levels[8:]]
    for first in range(0, centroids.shape[0], 512):
        table[first : first + 512, :] = product(centroids[first : first + 512, :], spread[...])
    first_half = lax.broadcasted_iota(jnp.int32, (8, DIM), 1) < DIM // 2
    doc_row = lax.broadcasted_iota(jnp.int32, (8, DIM), 0)
    scalars[0].wait()
    row_bits = [jnp.bitwise_and(doc_row, bit) != 0 for bit in (1, 2, 4)]

    def fetch(slot, first):
        rows = []
        for n in range(first, first + 8):
            row = table[pl.ds(ids[0, n * slots + slot], 1), :]
            rows.append(jnp.broadcast_to(row, (8, DIM)))
        for bit in row_bits:
            rows = [jnp.where(bit, rows[i + 1], rows[i]) for i in range(0, len(rows), 2)]
        return rows[0]

    def one_pair(pair, carry):
        start = pl.multiple_of(pair * docs, docs)
        column = pl.multiple_of(pair * DIM, DIM)
        parts = [[], []]
        for b in range(0, docs, 8):
            code = codes[b : b + 8, pl.ds(column, DIM)]
            other = pltpu.roll(code, DIM // 2, 1)
            nibbles = (
                jnp.where(first_half, jnp.bitwise_and(code, 15), jnp.right_shift(other, 4)),
                jnp.where(first_half, jnp.bitwise_and(other, 15), jnp.right_shift(code, 4)),
            )
            for k in range(2):
                parts[k].append(fetch(2 * pair + k, b) + look_up(nibbles[k], halves))
        for k, part in enumerate(parts):
            columns = slice(k * DIM, (k + 1) * DIM)
            left[pl.ds(start, docs), columns] = jnp.concatenate(part, axis=0).astype(jnp.bfloat16)
        return carry

    lax.fori_loop(0, pairs, one_pair, 0, unroll=True)
    scalars[1].wait()
    for b in range(docs // 8):
        block = jnp.zeros((8, DIM), jnp.int32)
        for n in range(8):
            block = jnp.where(doc_row == n, counts[0, b * 8 + n], block)
        live[b * 8 : b * 8 + 8, :] = block
    for copy in late:
        copy.wait()


def prepare(ids, counts, codes, centroids, buckets, spread, kept):
    docs, columns = codes.shape
    pairs = columns // DIM
    shape = jax.ShapeDtypeStruct
    return pl.pallas_call(
        functools.partial(prepare_kernel, len(kept)),
        out_shape=[
            shape((pairs * docs, 2 * DIM), jnp.bfloat16),
            shape((docs, DIM), jnp.int32),
        ]
        + [shape(array.shape, array.dtype) for array in kept],
        in_specs=[vmem()] * 5 + [hbm()] * (1 + len(kept)),
        out_specs=[vmem()] * (2 + len(kept)),
        scratch_shapes=[
            pltpu.SMEM(ids.shape, jnp.int32),
            pltpu.SMEM(counts.shape, jnp.int32),
            pltpu.VMEM(centroids.shape, jnp.float32),
            pltpu.SemaphoreType.DMA((2,)),
            pltpu.SemaphoreType.DMA((len(kept),)),
        ],
        compiler_params=pltpu.CompilerParams(vmem_limit_bytes=24 * 2**20),
        cost_estimate=pl.CostEstimate(flops=4 * 10**9, bytes_accessed=2**22, transcendentals=0),
        name="prepare",
    )(ids, codes, centroids, buckets, spread, *[in_hbm(x) for x in (counts, *kept)])


def tables_kernel(candidates_vmem, proj, _, chosen, proj_parts, candidates, sem):
    cand = candidates.shape[1]
    rows_dev = chosen.shape[0] - cand
    copy = pltpu.make_async_copy(candidates_vmem, candidates, sem)
    copy.start()
    parts = three_parts(proj[...])
    for i, k in enumerate(PART_PAIRS):
        proj_parts[i * QT : (i + 1) * QT, :] = parts[k[1]]

    copy.wait()
    docs_all = chosen.shape[1]
    member = lax.axis_index(MEMBERS)
    doc = lax.broadcasted_iota(jnp.int32, (16, docs_all), 1)
    place_in = lax.broadcasted_iota(jnp.int32, (16, docs_all), 0)

    def choose(i, carry):
        start = pl.multiple_of(i * 16, 16)
        source = jnp.where(start < cand, start, start - cand + member * rows_dev)
        wanted = jnp.zeros((16, docs_all), jnp.int32)
        for n in range(16):
            wanted = jnp.where(place_in == n, candidates[0, source + n], wanted)
        chosen[pl.ds(start, 16), :] = jnp.where(doc == wanted, 1.0, 0.0).astype(jnp.bfloat16)
        return carry

    lax.fori_loop(0, chosen.shape[0] // 16, choose, 0)


def make_tables(candidates, input_proj, best, docs_all, rows):
    shape = jax.ShapeDtypeStruct
    return pl.pallas_call(
        tables_kernel,
        out_shape=[
            shape((candidates.shape[1] + rows, docs_all), jnp.bfloat16),
            shape((len(PART_PAIRS) * QT, H), jnp.bfloat16),
        ],
        in_specs=[vmem(), vmem(), pl.BlockSpec(memory_space=pl.ANY)],
        out_specs=[vmem()] * 2,
        scratch_shapes=[pltpu.SMEM(candidates.shape, jnp.int32), pltpu.SemaphoreType.DMA],
        compiler_params=pltpu.CompilerParams(vmem_limit_bytes=16 * 2**20),
        cost_estimate=pl.CostEstimate(flops=5 * 10**8, bytes_accessed=0, transcendentals=0),
        name="make_tables",
    )(candidates, input_proj, best)


def score_kernel(sources, docs, left, live, spread, *refs):
    pieces, (out_ref, queries, right) = refs[: len(sources)], refs[len(sources) :]
    query_rows = queries.shape[0]
    pairs = left.shape[0] // docs
    place(pieces, sources, queries, MEMBERS)
    query_bf = queries[...].astype(jnp.bfloat16)
    query_bf = product(query_bf, spread[...]).astype(jnp.bfloat16)
    none = jnp.zeros((query_rows, DIM), jnp.bfloat16)
    right[:query_rows, :DIM] = query_bf
    right[:query_rows, DIM:] = none
    right[query_rows:, :DIM] = none
    right[query_rows:, DIM:] = query_bf

    counts = jnp.concatenate([live[...]] * (query_rows // DIM), axis=1)
    block = pairs if query_rows == DIM else 4

    def score(i, best):
        start = pl.multiple_of(i * block * docs, block * docs)
        scores = lax.dot_general(
            left[pl.ds(start, block * docs), :],
            right[...],
            (((1,), (1,)), ((), ())),
            preferred_element_type=jnp.float32,
        )
        for k in range(block):
            slot = 2 * (i * block + k)
            rows = scores[k * docs : (k + 1) * docs]
            best = jnp.maximum(best, jnp.where(counts > slot, rows[:, :query_rows], NOTHING))
            best = jnp.maximum(best, jnp.where(counts > slot + 1, rows[:, query_rows:], NOTHING))
        return best

    best = jnp.full((docs, query_rows), NOTHING, jnp.float32)
    if block == pairs:
        out_ref[...] = score(0, best)
    else:
        out_ref[...] = lax.fori_loop(0, pairs // block, score, best)


def local_maxima(left, live, spread, pieces, sources):
    docs = live.shape[0]
    query_rows = sum(piece.shape[0] for piece in pieces)
    return pl.pallas_call(
        functools.partial(score_kernel, sources, docs),
        out_shape=jax.ShapeDtypeStruct((docs, query_rows), jnp.float32),
        in_specs=[vmem()] * (3 + len(pieces)),
        out_specs=vmem(),
        scratch_shapes=[
            pltpu.VMEM((query_rows, DIM), jnp.float32),
            pltpu.VMEM((2 * query_rows, 2 * DIM), jnp.bfloat16),
        ],
        compiler_params=pltpu.CompilerParams(vmem_limit_bytes=24 * 2**20),
        name="local_maxima",
    )(left, live, spread, *pieces)


def rms_scale(values, gain):
    mean_square = jnp.mean(values * values, axis=-1, keepdims=True)
    return (values * lax.rsqrt(mean_square + 1e-06) * gain).astype(jnp.bfloat16)


def rerank_kernel(sources, *refs):
    pieces, refs = refs[: len(sources)], refs[len(sources) :]
    (
        chosen,
        proj_parts,
        gain_one,
        query_proj,
        key_proj,
        value_proj,
        output_proj,
        gain_two,
        up_proj,
        down_proj,
        out_ref,
        maxima,
    ) = refs
    rows = out_ref.shape[0]
    cand = chosen.shape[0] - rows
    place(pieces, sources, maxima, ("docs", "cent", "sub"))

    width = maxima.shape[1]
    own = pltpu.roll(maxima[...], lax.rem(width - lax.axis_index("docs") * QT, width), 1)
    parts = three_parts(own[:, :QT])
    stacked = jnp.concatenate([parts[k[0]] for k in PART_PAIRS], axis=1)
    features = product(chosen[...], stacked).astype(jnp.bfloat16)
    all_hidden = product(features, proj_parts[...])
    hidden_zero = all_hidden[cand:]
    normed = rms_scale(all_hidden, gain_one[...])
    query_heads = product(normed[cand:], query_proj[...]).astype(jnp.bfloat16)
    key_heads = product(normed[:cand], key_proj[...]).astype(jnp.bfloat16)
    value_heads = product(normed[:cand], value_proj[...]).astype(jnp.bfloat16)

    head_of = jnp.right_shift(lax.broadcasted_iota(jnp.int32, (rows, H), 1), 6)
    split = [jnp.where(head_of == h, query_heads, jnp.zeros_like(query_heads)) for h in range(HEADS)]
    scores = lax.dot_general(
        jnp.concatenate(split, axis=0),
        key_heads,
        (((1,), (1,)), ((), ())),
        preferred_element_type=jnp.float32,
    ) * (HEAD ** (-0.5))
    expon = jnp.exp(scores - jnp.max(scores, axis=-1, keepdims=True))
    summed = jnp.sum(expon, axis=-1, keepdims=True)
    spread = product(expon.astype(jnp.bfloat16), value_heads) / summed
    attended = spread[:rows]
    for h in range(1, HEADS):
        attended = jnp.where(head_of == h, spread[h * rows : (h + 1) * rows], attended)
    hidden_one = hidden_zero + product(attended.astype(jnp.bfloat16), output_proj[...])
    normed_two = rms_scale(hidden_one, gain_two[...])
    inner = jax.nn.gelu(product(normed_two, up_proj[...])).astype(jnp.bfloat16)
    out_ref[...] = hidden_one + product(inner, down_proj[...])


def rerank(pieces, sources, arrays, rows):
    docs_all = sum(piece.shape[0] for piece in pieces)
    query_rows = pieces[0].shape[1]
    return pl.pallas_call(
        functools.partial(rerank_kernel, sources),
        out_shape=jax.ShapeDtypeStruct((rows, H), jnp.float32),
        in_specs=[vmem()] * (len(pieces) + len(arrays)),
        out_specs=vmem(),
        scratch_shapes=[pltpu.VMEM((docs_all, query_rows), jnp.float32)],
        compiler_params=pltpu.CompilerParams(vmem_limit_bytes=32 * 2**20),
        name="rerank",
    )(*pieces, *arrays)


def on_device(
    queries,
    token_codes,
    centroid_ids,
    slot_counts,
    centroids,
    bucket_values,
    candidates,
    input_proj,
    gain_one,
    query_proj,
    key_proj,
    value_proj,
    output_proj,
    gain_two,
    up_proj,
    down_proj,
):
    kept = (
        gain_one[None, :],
        query_proj,
        key_proj,
        value_proj,
        output_proj,
        gain_two[None, :],
        up_proj,
        down_proj,
    )
    docs_all = slot_counts.shape[1] * lax.axis_size("docs")
    rows = candidates.shape[1] // lax.axis_size(MEMBERS)
    query_pieces, query_sources = gather_queries(queries)
    spread = early()
    left, live, *staged = prepare(
        centroid_ids, slot_counts, token_codes[0], centroids, bucket_values, spread, kept
    )
    local_best = local_maxima(left, live, spread, query_pieces, query_sources)
    tables = make_tables(candidates, input_proj, local_best, docs_all, rows)
    doc_pieces, doc_sources = gather_docs(best_of_members(local_best))
    return rerank(doc_pieces, doc_sources, [*tables, *staged], rows)[None]


def solution(mesh):
    in_specs = (
        P(("groups", "cent", "sub"), None),
        P(("cent", "sub"), ("groups", "docs"), None),
        P(("cent", "sub"), ("groups", "docs")),
        P(("cent", "sub"), ("groups", "docs")),
        P(("cent", "sub"), None),
        P(),
        P(("groups", "docs"), None),
        P(),
        P(),
        P(),
        P(),
        P(),
        P(),
        P(),
        P(),
        P(),
    )
    out_specs = P(("groups", "docs"), ("cent", "sub"), None)
    return jax.shard_map(
        on_device, mesh=mesh, in_specs=in_specs, out_specs=out_specs, check_vma=False
    )
```

```python
import functools

import jax
import jax.numpy as jnp
from jax import lax
from jax.experimental import pallas as pl
from jax.experimental.pallas import tpu as pltpu
from jax.sharding import PartitionSpec as P

DIM = 128
QT = 32
H = 256
HEADS = 4
HEAD = 64
MEMBERS = ("cent", "sub")
NOTHING = -1e30
PARTS = 3
QUERY_STEPS = ((2, 3, 1, 0), (1, 0, 3, 2), (3, 2, 0, 1))
FIRST_STEP = (4, 9, 11, 6, 8, 13, 10, 15, 12, 0, 2, 14, 5, 1, 7, 3)
SECOND_STEP = (13, 12, 15, 14, 0, 1, 3, 2, 5, 4, 6, 7, 10, 8, 11, 9)


def compact():
    return (
        lax.axis_size("cent") == 2
        and lax.axis_size("sub") == 2
        and 4 * lax.axis_size("docs") == len(SECOND_STEP)
    )


def gather_queries(queries):
    if not compact():
        return [lax.all_gather(queries, MEMBERS, axis=0, tiled=True)], [None]
    pieces, sources = [queries], [[0, 1, 2, 3]]
    for step in QUERY_STEPS:
        sources.append([step.index(i) for i in range(4)])
        pieces.append(lax.ppermute(queries, MEMBERS, list(enumerate(step))))
    return pieces, sources


def best_of_members(values):
    if not compact():
        return lax.pmax(values, MEMBERS)
    values = jnp.maximum(values, lax.ppermute(values, "sub", [(0, 1), (1, 0)]))
    return jnp.maximum(values, lax.ppermute(values, MEMBERS, [(i, i ^ 3) for i in range(4)]))


def gather_docs(values):
    if not compact():
        return [lax.all_gather(values, "docs", axis=0, tiled=True)], [None]
    axes = ("docs", "cent", "sub")
    first = lax.ppermute(values, axes, list(enumerate(FIRST_STEP)))
    second = lax.ppermute(values, axes, list(enumerate(SECOND_STEP)))
    other = lax.ppermute(first, "sub", [(0, 1), (1, 0)])
    places = range(len(FIRST_STEP))
    sources = [
        [i // 4 for i in places],
        [FIRST_STEP.index(i) // 4 for i in places],
        [FIRST_STEP.index(i ^ 1) // 4 for i in places],
        [SECOND_STEP.index(i) // 4 for i in places],
    ]
    return [values, first, other, second], sources


def place(pieces, sources, out_ref, axes):
    if len(pieces) == 1:
        out_ref[...] = pieces[0][...].astype(out_ref.dtype)
        return
    me = lax.axis_index(axes)
    for piece, source in zip(pieces, sources):
        rows = piece.shape[0]
        place_of = jnp.int32(source[0])
        for i in range(1, len(source)):
            place_of = jnp.where(me == i, source[i], place_of)
        start = pl.multiple_of(place_of * rows, rows)
        out_ref[pl.ds(start, rows), :] = piece[...].astype(out_ref.dtype)


def vmem():
    return pl.BlockSpec(memory_space=pltpu.VMEM)


def smem():
    return pl.BlockSpec(memory_space=pltpu.SMEM)


def hbm():
    return pl.BlockSpec(memory_space=pltpu.HBM)


def in_hbm(array):
    return pltpu.with_memory_space_constraint(array, pltpu.HBM)


def even_odd_columns():
    column = lax.broadcasted_iota(jnp.int32, (DIM, DIM), 1)
    dim = lax.broadcasted_iota(jnp.int32, (DIM, DIM), 0)
    wanted = 2 * jnp.bitwise_and(column, 63) + jnp.right_shift(column, 6)
    return jnp.where(wanted == dim, 1.0, 0.0).astype(jnp.bfloat16)


def product(left, right):
    return jnp.dot(left, right, preferred_element_type=jnp.float32)


def three_parts(values):
    parts = []
    for _ in range(PARTS):
        part = values.astype(jnp.bfloat16)
        values = values - part.astype(jnp.float32)
        parts.append(part)
    return parts


def look_up(nibbles, halves):
    index = jnp.bitwise_and(nibbles, 7)
    lower = jnp.take_along_axis(halves[0], index, axis=0)
    upper = jnp.take_along_axis(halves[1], index, axis=0)
    return jnp.where(nibbles >= 8, upper, lower)


def early_kernel(spread):
    spread[...] = even_odd_columns()


def early():
    return pl.pallas_call(
        early_kernel,
        out_shape=jax.ShapeDtypeStruct((DIM, DIM), jnp.bfloat16),
        out_specs=vmem(),
        compiler_params=pltpu.CompilerParams(vmem_limit_bytes=4 * 2**20),
        cost_estimate=pl.CostEstimate(flops=4 * 10**9, bytes_accessed=0, transcendentals=0),
        name="early",
    )()


def prepare_kernel(n_kept, ids_vmem, codes, centroids, buckets, spread, counts_hbm, *refs):
    kept_hbm, (left, live), refs = refs[:n_kept], refs[n_kept : n_kept + 2], refs[n_kept + 2 :]
    kept, (ids, counts, table, sems, kept_sems) = refs[:n_kept], refs[n_kept:]
    docs, columns = codes.shape
    pairs = columns // DIM
    slots = 2 * pairs
    scalars = [
        pltpu.make_async_copy(source, target, sems.at[i])
        for i, (source, target) in enumerate(((ids_vmem, ids), (counts_hbm, counts)))
    ]
    late = [
        pltpu.make_async_copy(source, target, kept_sems.at[i])
        for i, (source, target) in enumerate(zip(kept_hbm, kept))
    ]
    for copy in scalars + late:
        copy.start()
    levels = sum(product(part, spread[...]) for part in three_parts(buckets[...]))
    halves = [levels[:8], levels[8:]]
    for first in range(0, centroids.shape[0], 512):
        table[first : first + 512, :] = product(centroids[first : first + 512, :], spread[...])
    first_half = lax.broadcasted_iota(jnp.int32, (8, DIM), 1) < DIM // 2
    doc_row = lax.broadcasted_iota(jnp.int32, (8, DIM), 0)
    scalars[0].wait()
    row_bits = [jnp.bitwise_and(doc_row, bit) != 0 for bit in (1, 2, 4)]

    def fetch(slot, first):
        rows = []
        for n in range(first, first + 8):
            row = table[pl.ds(ids[0, n * slots + slot], 1), :]
            rows.append(jnp.broadcast_to(row, (8, DIM)))
        for bit in row_bits:
            rows = [jnp.where(bit, rows[i + 1], rows[i]) for i in range(0, len(rows), 2)]
        return rows[0]

    def one_pair(pair, carry):
        start = pl.multiple_of(pair * docs, docs)
        column = pl.multiple_of(pair * DIM, DIM)
        parts = [[], []]
        for b in range(0, docs, 8):
            code = codes[b : b + 8, pl.ds(column, DIM)]
            other = pltpu.roll(code, DIM // 2, 1)
            nibbles = (
                jnp.where(first_half, jnp.bitwise_and(code, 15), jnp.right_shift(other, 4)),
                jnp.where(first_half, jnp.bitwise_and(other, 15), jnp.right_shift(code, 4)),
            )
            for k in range(2):
                parts[k].append(fetch(2 * pair + k, b) + look_up(nibbles[k], halves))
        for k, part in enumerate(parts):
            columns = slice(k * DIM, (k + 1) * DIM)
            left[pl.ds(start, docs), columns] = jnp.concatenate(part, axis=0).astype(jnp.bfloat16)
        return carry

    lax.fori_loop(0, pairs, one_pair, 0, unroll=True)
    scalars[1].wait()
    for b in range(docs // 8):
        block = jnp.zeros((8, DIM), jnp.int32)
        for n in range(8):
            block = jnp.where(doc_row == n, counts[0, b * 8 + n], block)
        live[b * 8 : b * 8 + 8, :] = block
    for copy in late:
        copy.wait()


def prepare(ids, counts, codes, centroids, buckets, spread, kept):
    docs, columns = codes.shape
    pairs = columns // DIM
    shape = jax.ShapeDtypeStruct
    return pl.pallas_call(
        functools.partial(prepare_kernel, len(kept)),
        out_shape=[
            shape((pairs * docs, 2 * DIM), jnp.bfloat16),
            shape((docs, DIM), jnp.int32),
        ]
        + [shape(array.shape, array.dtype) for array in kept],
        in_specs=[vmem()] * 5 + [hbm()] * (1 + len(kept)),
        out_specs=[vmem()] * (2 + len(kept)),
        scratch_shapes=[
            pltpu.SMEM(ids.shape, jnp.int32),
            pltpu.SMEM(counts.shape, jnp.int32),
            pltpu.VMEM(centroids.shape, jnp.float32),
            pltpu.SemaphoreType.DMA((2,)),
            pltpu.SemaphoreType.DMA((len(kept),)),
        ],
        compiler_params=pltpu.CompilerParams(vmem_limit_bytes=24 * 2**20),
        cost_estimate=pl.CostEstimate(flops=4 * 10**9, bytes_accessed=2**22, transcendentals=0),
        name="prepare",
    )(ids, codes, centroids, buckets, spread, *[in_hbm(x) for x in (counts, *kept)])


def tables_kernel(candidates_vmem, proj, _, chosen, proj_parts, candidates, sem):
    cand = candidates.shape[1]
    rows_dev = chosen.shape[0] - cand
    copy = pltpu.make_async_copy(candidates_vmem, candidates, sem)
    copy.start()
    parts = three_parts(proj[...])
    for i, part in enumerate(parts):
        proj_parts[i * QT : (i + 1) * QT, :] = part

    copy.wait()
    docs_all = chosen.shape[1]
    member = lax.axis_index(MEMBERS)
    doc = lax.broadcasted_iota(jnp.int32, (16, docs_all), 1)
    place_in = lax.broadcasted_iota(jnp.int32, (16, docs_all), 0)

    def choose(i, carry):
        start = pl.multiple_of(i * 16, 16)
        source = jnp.where(start < cand, start, start - cand + member * rows_dev)
        wanted = jnp.zeros((16, docs_all), jnp.int32)
        for n in range(16):
            wanted = jnp.where(place_in == n, candidates[0, source + n], wanted)
        chosen[pl.ds(start, 16), :] = jnp.where(doc == wanted, 1.0, 0.0).astype(jnp.bfloat16)
        return carry

    lax.fori_loop(0, chosen.shape[0] // 16, choose, 0)


def make_tables(candidates, input_proj, best, docs_all, rows):
    shape = jax.ShapeDtypeStruct
    return pl.pallas_call(
        tables_kernel,
        out_shape=[
            shape((candidates.shape[1] + rows, docs_all), jnp.bfloat16),
            shape((PARTS * QT, H), jnp.bfloat16),
        ],
        in_specs=[vmem(), vmem(), pl.BlockSpec(memory_space=pl.ANY)],
        out_specs=[vmem()] * 2,
        scratch_shapes=[pltpu.SMEM(candidates.shape, jnp.int32), pltpu.SemaphoreType.DMA],
        compiler_params=pltpu.CompilerParams(vmem_limit_bytes=16 * 2**20),
        cost_estimate=pl.CostEstimate(flops=5 * 10**8, bytes_accessed=0, transcendentals=0),
        name="make_tables",
    )(candidates, input_proj, best)


def score_kernel(sources, docs, left, live, spread, *refs):
    pieces, (out_ref, queries, right) = refs[: len(sources)], refs[len(sources) :]
    query_rows = queries.shape[0]
    pairs = left.shape[0] // docs
    place(pieces, sources, queries, MEMBERS)
    query_bf = queries[...].astype(jnp.bfloat16)
    query_bf = product(query_bf, spread[...]).astype(jnp.bfloat16)
    none = jnp.zeros((query_rows, DIM), jnp.bfloat16)
    right[:query_rows, :DIM] = query_bf
    right[:query_rows, DIM:] = none
    right[query_rows:, :DIM] = none
    right[query_rows:, DIM:] = query_bf

    counts = jnp.concatenate([live[...]] * (query_rows // DIM), axis=1)
    block = pairs if query_rows == DIM else 4

    def score(i, best):
        start = pl.multiple_of(i * block * docs, block * docs)
        scores = lax.dot_general(
            left[pl.ds(start, block * docs), :],
            right[...],
            (((1,), (1,)), ((), ())),
            preferred_element_type=jnp.float32,
        )
        for k in range(block):
            slot = 2 * (i * block + k)
            rows = scores[k * docs : (k + 1) * docs]
            best = jnp.maximum(best, jnp.where(counts > slot, rows[:, :query_rows], NOTHING))
            best = jnp.maximum(best, jnp.where(counts > slot + 1, rows[:, query_rows:], NOTHING))
        return best

    best = jnp.full((docs, query_rows), NOTHING, jnp.float32)
    if block == pairs:
        out_ref[...] = score(0, best).astype(out_ref.dtype)
    else:
        out_ref[...] = lax.fori_loop(0, pairs // block, score, best).astype(out_ref.dtype)


def local_maxima(left, live, spread, pieces, sources):
    docs = live.shape[0]
    query_rows = sum(piece.shape[0] for piece in pieces)
    return pl.pallas_call(
        functools.partial(score_kernel, sources, docs),
        out_shape=jax.ShapeDtypeStruct((docs, query_rows), jnp.bfloat16),
        in_specs=[vmem()] * (3 + len(pieces)),
        out_specs=vmem(),
        scratch_shapes=[
            pltpu.VMEM((query_rows, DIM), jnp.float32),
            pltpu.VMEM((2 * query_rows, 2 * DIM), jnp.bfloat16),
        ],
        compiler_params=pltpu.CompilerParams(vmem_limit_bytes=24 * 2**20),
        name="local_maxima",
    )(left, live, spread, *pieces)


def rms_scale(values, gain):
    mean_square = jnp.mean(values * values, axis=-1, keepdims=True)
    return (values * lax.rsqrt(mean_square + 1e-06) * gain).astype(jnp.bfloat16)


def rerank_kernel(sources, *refs):
    pieces, refs = refs[: len(sources)], refs[len(sources) :]
    (
        chosen,
        proj_parts,
        gain_one,
        query_proj,
        key_proj,
        value_proj,
        output_proj,
        gain_two,
        up_proj,
        down_proj,
        out_ref,
        maxima,
    ) = refs
    rows = out_ref.shape[0]
    cand = chosen.shape[0] - rows
    place(pieces, sources, maxima, ("docs", "cent", "sub"))

    width = maxima.shape[1]
    own = pltpu.roll(maxima[...], lax.rem(width - lax.axis_index("docs") * QT, width), 1)
    stacked = jnp.concatenate([own[:, :QT].astype(jnp.bfloat16)] * PARTS, axis=1)
    features = product(chosen[...], stacked).astype(jnp.bfloat16)
    all_hidden = product(features, proj_parts[...])
    hidden_zero = all_hidden[cand:]
    normed = rms_scale(all_hidden, gain_one[...])
    query_heads = product(normed[cand:], query_proj[...]).astype(jnp.bfloat16)
    key_heads = product(normed[:cand], key_proj[...]).astype(jnp.bfloat16)
    value_heads = product(normed[:cand], value_proj[...]).astype(jnp.bfloat16)

    head_of = jnp.right_shift(lax.broadcasted_iota(jnp.int32, (rows, H), 1), 6)
    split = [jnp.where(head_of == h, query_heads, jnp.zeros_like(query_heads)) for h in range(HEADS)]
    scores = lax.dot_general(
        jnp.concatenate(split, axis=0),
        key_heads,
        (((1,), (1,)), ((), ())),
        preferred_element_type=jnp.float32,
    ) * (HEAD ** (-0.5))
    expon = jnp.exp(scores - jnp.max(scores, axis=-1, keepdims=True))
    summed = jnp.sum(expon, axis=-1, keepdims=True)
    spread = product(expon.astype(jnp.bfloat16), value_heads) / summed
    attended = spread[:rows]
    for h in range(1, HEADS):
        attended = jnp.where(head_of == h, spread[h * rows : (h + 1) * rows], attended)
    hidden_one = hidden_zero + product(attended.astype(jnp.bfloat16), output_proj[...])
    normed_two = rms_scale(hidden_one, gain_two[...])
    inner = jax.nn.gelu(product(normed_two, up_proj[...])).astype(jnp.bfloat16)
    out_ref[...] = hidden_one + product(inner, down_proj[...])


def rerank(pieces, sources, arrays, rows):
    docs_all = sum(piece.shape[0] for piece in pieces)
    query_rows = pieces[0].shape[1]
    return pl.pallas_call(
        functools.partial(rerank_kernel, sources),
        out_shape=jax.ShapeDtypeStruct((rows, H), jnp.float32),
        in_specs=[vmem()] * (len(pieces) + len(arrays)),
        out_specs=vmem(),
        scratch_shapes=[pltpu.VMEM((docs_all, query_rows), jnp.float32)],
        compiler_params=pltpu.CompilerParams(vmem_limit_bytes=32 * 2**20),
        name="rerank",
    )(*pieces, *arrays)


def on_device(
    queries,
    token_codes,
    centroid_ids,
    slot_counts,
    centroids,
    bucket_values,
    candidates,
    input_proj,
    gain_one,
    query_proj,
    key_proj,
    value_proj,
    output_proj,
    gain_two,
    up_proj,
    down_proj,
):
    kept = (
        gain_one[None, :],
        query_proj,
        key_proj,
        value_proj,
        output_proj,
        gain_two[None, :],
        up_proj,
        down_proj,
    )
    docs_all = slot_counts.shape[1] * lax.axis_size("docs")
    rows = candidates.shape[1] // lax.axis_size(MEMBERS)
    query_pieces, query_sources = gather_queries(queries)
    spread = early()
    left, live, *staged = prepare(
        centroid_ids, slot_counts, token_codes[0], centroids, bucket_values, spread, kept
    )
    local_best = local_maxima(left, live, spread, query_pieces, query_sources)
    tables = make_tables(candidates, input_proj, local_best, docs_all, rows)
    doc_pieces, doc_sources = gather_docs(best_of_members(local_best))
    return rerank(doc_pieces, doc_sources, [*tables, *staged], rows)[None]


def solution(mesh):
    in_specs = (
        P(("groups", "cent", "sub"), None),
        P(("cent", "sub"), ("groups", "docs"), None),
        P(("cent", "sub"), ("groups", "docs")),
        P(("cent", "sub"), ("groups", "docs")),
        P(("cent", "sub"), None),
        P(),
        P(("groups", "docs"), None),
        P(),
        P(),
        P(),
        P(),
        P(),
        P(),
        P(),
        P(),
        P(),
    )
    out_specs = P(("groups", "docs"), ("cent", "sub"), None)
    return jax.shard_map(
        on_device, mesh=mesh, in_specs=in_specs, out_specs=out_specs, check_vma=False
    )
```

```python
import functools

import jax
import jax.numpy as jnp
from jax import lax
from jax.experimental import pallas as pl
from jax.experimental.pallas import tpu as pltpu
from jax.sharding import PartitionSpec as P

DIM = 128
QT = 32
H = 256
HEADS = 4
HEAD = 64
MEMBERS = ("cent", "sub")
NOTHING = -1e30
PARTS = 3
QUERY_STEPS = ((2, 3, 1, 0), (1, 0, 3, 2), (3, 2, 0, 1))
FIRST_STEP = (4, 9, 11, 6, 8, 13, 10, 15, 12, 0, 2, 14, 5, 1, 7, 3)
SECOND_STEP = (13, 12, 15, 14, 0, 1, 3, 2, 5, 7, 6, 4, 10, 8, 11, 9)
NEIGHBOUR_STEP = (3, 2, 1, 0, 6, 7, 5, 4, 11, 10, 9, 8, 15, 14, 12, 13)


def compact():
    return (
        lax.axis_size("cent") == 2
        and lax.axis_size("sub") == 2
        and 4 * lax.axis_size("docs") == len(SECOND_STEP)
    )


def gather_queries(queries):
    if not compact():
        return [lax.all_gather(queries, MEMBERS, axis=0, tiled=True)], [None]
    pieces, sources = [queries], [[0, 1, 2, 3]]
    for step in QUERY_STEPS:
        sources.append([step.index(i) for i in range(4)])
        pieces.append(lax.ppermute(queries, MEMBERS, list(enumerate(step))))
    return pieces, sources


def best_of_members(values):
    if not compact():
        return lax.pmax(values, MEMBERS)
    values = jnp.maximum(values, lax.ppermute(values, "sub", [(0, 1), (1, 0)]))
    axes = ("docs", "cent", "sub")
    return jnp.maximum(values, lax.ppermute(values, axes, list(enumerate(NEIGHBOUR_STEP))))


def gather_docs(values):
    if not compact():
        return [lax.all_gather(values, "docs", axis=0, tiled=True)], [None]
    axes = ("docs", "cent", "sub")
    first = lax.ppermute(values, axes, list(enumerate(FIRST_STEP)))
    second = lax.ppermute(values, axes, list(enumerate(SECOND_STEP)))
    other = lax.ppermute(first, "sub", [(0, 1), (1, 0)])
    places = range(len(FIRST_STEP))
    sources = [
        [i // 4 for i in places],
        [FIRST_STEP.index(i) // 4 for i in places],
        [FIRST_STEP.index(i ^ 1) // 4 for i in places],
        [SECOND_STEP.index(i) // 4 for i in places],
    ]
    return [values, first, other, second], sources


def place(pieces, sources, out_ref, axes):
    if len(pieces) == 1:
        out_ref[...] = pieces[0][...].astype(out_ref.dtype)
        return
    me = lax.axis_index(axes)
    for piece, source in zip(pieces, sources):
        rows = piece.shape[0]
        place_of = jnp.int32(source[0])
        for i in range(1, len(source)):
            place_of = jnp.where(me == i, source[i], place_of)
        start = pl.multiple_of(place_of * rows, rows)
        out_ref[pl.ds(start, rows), :] = piece[...].astype(out_ref.dtype)


def vmem():
    return pl.BlockSpec(memory_space=pltpu.VMEM)


def smem():
    return pl.BlockSpec(memory_space=pltpu.SMEM)


def hbm():
    return pl.BlockSpec(memory_space=pltpu.HBM)


def in_hbm(array):
    return pltpu.with_memory_space_constraint(array, pltpu.HBM)


def even_odd_columns():
    column = lax.broadcasted_iota(jnp.int32, (DIM, DIM), 1)
    dim = lax.broadcasted_iota(jnp.int32, (DIM, DIM), 0)
    wanted = 2 * jnp.bitwise_and(column, 63) + jnp.right_shift(column, 6)
    return jnp.where(wanted == dim, 1.0, 0.0).astype(jnp.bfloat16)


def product(left, right):
    return jnp.dot(left, right, preferred_element_type=jnp.float32)


def three_parts(values):
    parts = []
    for _ in range(PARTS):
        part = values.astype(jnp.bfloat16)
        values = values - part.astype(jnp.float32)
        parts.append(part)
    return parts


def look_up(nibbles, halves):
    index = jnp.bitwise_and(nibbles, 7)
    lower = jnp.take_along_axis(halves[0], index, axis=0)
    upper = jnp.take_along_axis(halves[1], index, axis=0)
    return jnp.where(nibbles >= 8, upper, lower)


def early_kernel(spread):
    spread[...] = even_odd_columns()


def early():
    return pl.pallas_call(
        early_kernel,
        out_shape=jax.ShapeDtypeStruct((DIM, DIM), jnp.bfloat16),
        out_specs=vmem(),
        compiler_params=pltpu.CompilerParams(vmem_limit_bytes=4 * 2**20),
        cost_estimate=pl.CostEstimate(flops=4 * 10**9, bytes_accessed=0, transcendentals=0),
        name="early",
    )()


def prepare_kernel(n_kept, ids_vmem, codes, centroids, buckets, spread, counts_hbm, *refs):
    kept_hbm, (left, live), refs = refs[:n_kept], refs[n_kept : n_kept + 2], refs[n_kept + 2 :]
    kept, (ids, counts, table, sems, kept_sems) = refs[:n_kept], refs[n_kept:]
    docs, columns = codes.shape
    pairs = columns // DIM
    slots = 2 * pairs
    scalars = [
        pltpu.make_async_copy(source, target, sems.at[i])
        for i, (source, target) in enumerate(((ids_vmem, ids), (counts_hbm, counts)))
    ]
    late = [
        pltpu.make_async_copy(source, target, kept_sems.at[i])
        for i, (source, target) in enumerate(zip(kept_hbm, kept))
    ]
    for copy in scalars + late:
        copy.start()
    levels = sum(product(part, spread[...]) for part in three_parts(buckets[...]))
    halves = [levels[:8], levels[8:]]
    for first in range(0, centroids.shape[0], 512):
        table[first : first + 512, :] = product(centroids[first : first + 512, :], spread[...])
    first_half = lax.broadcasted_iota(jnp.int32, (8, DIM), 1) < DIM // 2
    doc_row = lax.broadcasted_iota(jnp.int32, (8, DIM), 0)
    scalars[0].wait()
    row_bits = [jnp.bitwise_and(doc_row, bit) != 0 for bit in (1, 2, 4)]

    def fetch(slot, first):
        rows = []
        for n in range(first, first + 8):
            row = table[pl.ds(ids[0, n * slots + slot], 1), :]
            rows.append(jnp.broadcast_to(row, (8, DIM)))
        for bit in row_bits:
            rows = [jnp.where(bit, rows[i + 1], rows[i]) for i in range(0, len(rows), 2)]
        return rows[0]

    def one_pair(pair, carry):
        start = pl.multiple_of(pair * docs, docs)
        column = pl.multiple_of(pair * DIM, DIM)
        parts = [[], []]
        for b in range(0, docs, 8):
            code = codes[b : b + 8, pl.ds(column, DIM)]
            other = pltpu.roll(code, DIM // 2, 1)
            nibbles = (
                jnp.where(first_half, jnp.bitwise_and(code, 15), jnp.right_shift(other, 4)),
                jnp.where(first_half, jnp.bitwise_and(other, 15), jnp.right_shift(code, 4)),
            )
            for k in range(2):
                parts[k].append(fetch(2 * pair + k, b) + look_up(nibbles[k], halves))
        for k, part in enumerate(parts):
            columns = slice(k * DIM, (k + 1) * DIM)
            left[pl.ds(start, docs), columns] = jnp.concatenate(part, axis=0).astype(jnp.bfloat16)
        return carry

    lax.fori_loop(0, pairs, one_pair, 0, unroll=True)
    scalars[1].wait()
    for b in range(docs // 8):
        block = jnp.zeros((8, DIM), jnp.int32)
        for n in range(8):
            block = jnp.where(doc_row == n, counts[0, b * 8 + n], block)
        live[b * 8 : b * 8 + 8, :] = block
    for copy in late:
        copy.wait()


def prepare(ids, counts, codes, centroids, buckets, spread, kept):
    docs, columns = codes.shape
    pairs = columns // DIM
    shape = jax.ShapeDtypeStruct
    return pl.pallas_call(
        functools.partial(prepare_kernel, len(kept)),
        out_shape=[
            shape((pairs * docs, 2 * DIM), jnp.bfloat16),
            shape((docs, DIM), jnp.int32),
        ]
        + [shape(array.shape, array.dtype) for array in kept],
        in_specs=[vmem()] * 5 + [hbm()] * (1 + len(kept)),
        out_specs=[vmem()] * (2 + len(kept)),
        scratch_shapes=[
            pltpu.SMEM(ids.shape, jnp.int32),
            pltpu.SMEM(counts.shape, jnp.int32),
            pltpu.VMEM(centroids.shape, jnp.float32),
            pltpu.SemaphoreType.DMA((2,)),
            pltpu.SemaphoreType.DMA((len(kept),)),
        ],
        compiler_params=pltpu.CompilerParams(vmem_limit_bytes=24 * 2**20),
        cost_estimate=pl.CostEstimate(flops=4 * 10**9, bytes_accessed=2**22, transcendentals=0),
        name="prepare",
    )(ids, codes, centroids, buckets, spread, *[in_hbm(x) for x in (counts, *kept)])


def tables_kernel(candidates_vmem, proj, _, chosen, proj_parts, candidates, sem):
    cand = candidates.shape[1]
    rows_dev = chosen.shape[0] - cand
    copy = pltpu.make_async_copy(candidates_vmem, candidates, sem)
    copy.start()
    parts = three_parts(proj[...])
    for i, part in enumerate(parts):
        proj_parts[i * QT : (i + 1) * QT, :] = part

    copy.wait()
    docs_all = chosen.shape[1]
    member = lax.axis_index(MEMBERS)
    doc = lax.broadcasted_iota(jnp.int32, (16, docs_all), 1)
    place_in = lax.broadcasted_iota(jnp.int32, (16, docs_all), 0)

    def choose(i, carry):
        start = pl.multiple_of(i * 16, 16)
        source = jnp.where(start < cand, start, start - cand + member * rows_dev)
        wanted = jnp.zeros((16, docs_all), jnp.int32)
        for n in range(16):
            wanted = jnp.where(place_in == n, candidates[0, source + n], wanted)
        chosen[pl.ds(start, 16), :] = jnp.where(doc == wanted, 1.0, 0.0).astype(jnp.bfloat16)
        return carry

    lax.fori_loop(0, chosen.shape[0] // 16, choose, 0)


def make_tables(candidates, input_proj, best, docs_all, rows):
    shape = jax.ShapeDtypeStruct
    return pl.pallas_call(
        tables_kernel,
        out_shape=[
            shape((candidates.shape[1] + rows, docs_all), jnp.bfloat16),
            shape((PARTS * QT, H), jnp.bfloat16),
        ],
        in_specs=[vmem(), vmem(), pl.BlockSpec(memory_space=pl.ANY)],
        out_specs=[vmem()] * 2,
        scratch_shapes=[pltpu.SMEM(candidates.shape, jnp.int32), pltpu.SemaphoreType.DMA],
        compiler_params=pltpu.CompilerParams(vmem_limit_bytes=16 * 2**20),
        cost_estimate=pl.CostEstimate(flops=5 * 10**8, bytes_accessed=0, transcendentals=0),
        name="make_tables",
    )(candidates, input_proj, best)


def score_kernel(sources, docs, left, live, spread, *refs):
    pieces, (out_ref, queries, right) = refs[: len(sources)], refs[len(sources) :]
    query_rows = queries.shape[0]
    pairs = left.shape[0] // docs
    place(pieces, sources, queries, MEMBERS)
    query_bf = queries[...].astype(jnp.bfloat16)
    query_bf = product(query_bf, spread[...]).astype(jnp.bfloat16)
    none = jnp.zeros((query_rows, DIM), jnp.bfloat16)
    right[:query_rows, :DIM] = query_bf
    right[:query_rows, DIM:] = none
    right[query_rows:, :DIM] = none
    right[query_rows:, DIM:] = query_bf

    counts = jnp.concatenate([live[...]] * (query_rows // DIM), axis=1)
    block = pairs if query_rows == DIM else 4

    def score(i, best):
        start = pl.multiple_of(i * block * docs, block * docs)
        scores = lax.dot_general(
            left[pl.ds(start, block * docs), :],
            right[...],
            (((1,), (1,)), ((), ())),
            preferred_element_type=jnp.float32,
        )
        for k in range(block):
            slot = 2 * (i * block + k)
            rows = scores[k * docs : (k + 1) * docs]
            best = jnp.maximum(best, jnp.where(counts > slot, rows[:, :query_rows], NOTHING))
            best = jnp.maximum(best, jnp.where(counts > slot + 1, rows[:, query_rows:], NOTHING))
        return best

    best = jnp.full((docs, query_rows), NOTHING, jnp.float32)
    if block == pairs:
        out_ref[...] = score(0, best).astype(out_ref.dtype)
    else:
        out_ref[...] = lax.fori_loop(0, pairs // block, score, best).astype(out_ref.dtype)


def local_maxima(left, live, spread, pieces, sources):
    docs = live.shape[0]
    query_rows = sum(piece.shape[0] for piece in pieces)
    return pl.pallas_call(
        functools.partial(score_kernel, sources, docs),
        out_shape=jax.ShapeDtypeStruct((docs, query_rows), jnp.bfloat16),
        in_specs=[vmem()] * (3 + len(pieces)),
        out_specs=vmem(),
        scratch_shapes=[
            pltpu.VMEM((query_rows, DIM), jnp.float32),
            pltpu.VMEM((2 * query_rows, 2 * DIM), jnp.bfloat16),
        ],
        compiler_params=pltpu.CompilerParams(vmem_limit_bytes=24 * 2**20),
        name="local_maxima",
    )(left, live, spread, *pieces)


def rms_scale(values, gain):
    mean_square = jnp.mean(values * values, axis=-1, keepdims=True)
    return (values * lax.rsqrt(mean_square + 1e-06) * gain).astype(jnp.bfloat16)


def rerank_kernel(sources, *refs):
    pieces, refs = refs[: len(sources)], refs[len(sources) :]
    (
        chosen,
        proj_parts,
        gain_one,
        query_proj,
        key_proj,
        value_proj,
        output_proj,
        gain_two,
        up_proj,
        down_proj,
        out_ref,
        maxima,
    ) = refs
    rows = out_ref.shape[0]
    cand = chosen.shape[0] - rows
    place(pieces, sources, maxima, ("docs", "cent", "sub"))

    width = maxima.shape[1]
    own = pltpu.roll(maxima[...], lax.rem(width - lax.axis_index("docs") * QT, width), 1)
    stacked = jnp.concatenate([own[:, :QT].astype(jnp.bfloat16)] * PARTS, axis=1)
    features = product(chosen[...], stacked).astype(jnp.bfloat16)
    all_hidden = product(features, proj_parts[...])
    hidden_zero = all_hidden[cand:]
    normed = rms_scale(all_hidden, gain_one[...])
    query_heads = product(normed[cand:], query_proj[...]).astype(jnp.bfloat16)
    key_heads = product(normed[:cand], key_proj[...]).astype(jnp.bfloat16)
    value_heads = product(normed[:cand], value_proj[...]).astype(jnp.bfloat16)

    head_of = jnp.right_shift(lax.broadcasted_iota(jnp.int32, (rows, H), 1), 6)
    split = [jnp.where(head_of == h, query_heads, jnp.zeros_like(query_heads)) for h in range(HEADS)]
    scores = lax.dot_general(
        jnp.concatenate(split, axis=0),
        key_heads,
        (((1,), (1,)), ((), ())),
        preferred_element_type=jnp.float32,
    ) * (HEAD ** (-0.5))
    expon = jnp.exp(scores - jnp.max(scores, axis=-1, keepdims=True))
    summed = jnp.sum(expon, axis=-1, keepdims=True)
    spread = product(expon.astype(jnp.bfloat16), value_heads) / summed
    attended = spread[:rows]
    for h in range(1, HEADS):
        attended = jnp.where(head_of == h, spread[h * rows : (h + 1) * rows], attended)
    hidden_one = hidden_zero + product(attended.astype(jnp.bfloat16), output_proj[...])
    normed_two = rms_scale(hidden_one, gain_two[...])
    inner = jax.nn.gelu(product(normed_two, up_proj[...])).astype(jnp.bfloat16)
    out_ref[...] = hidden_one + product(inner, down_proj[...])


def rerank(pieces, sources, arrays, rows):
    docs_all = sum(piece.shape[0] for piece in pieces)
    query_rows = pieces[0].shape[1]
    return pl.pallas_call(
        functools.partial(rerank_kernel, sources),
        out_shape=jax.ShapeDtypeStruct((rows, H), jnp.float32),
        in_specs=[vmem()] * (len(pieces) + len(arrays)),
        out_specs=vmem(),
        scratch_shapes=[pltpu.VMEM((docs_all, query_rows), jnp.float32)],
        compiler_params=pltpu.CompilerParams(vmem_limit_bytes=32 * 2**20),
        name="rerank",
    )(*pieces, *arrays)


def on_device(
    queries,
    token_codes,
    centroid_ids,
    slot_counts,
    centroids,
    bucket_values,
    candidates,
    input_proj,
    gain_one,
    query_proj,
    key_proj,
    value_proj,
    output_proj,
    gain_two,
    up_proj,
    down_proj,
):
    kept = (
        gain_one[None, :],
        query_proj,
        key_proj,
        value_proj,
        output_proj,
        gain_two[None, :],
        up_proj,
        down_proj,
    )
    docs_all = slot_counts.shape[1] * lax.axis_size("docs")
    rows = candidates.shape[1] // lax.axis_size(MEMBERS)
    query_pieces, query_sources = gather_queries(queries)
    spread = early()
    left, live, *staged = prepare(
        centroid_ids, slot_counts, token_codes[0], centroids, bucket_values, spread, kept
    )
    local_best = local_maxima(left, live, spread, query_pieces, query_sources)
    tables = make_tables(candidates, input_proj, local_best, docs_all, rows)
    doc_pieces, doc_sources = gather_docs(best_of_members(local_best))
    return rerank(doc_pieces, doc_sources, [*tables, *staged], rows)[None]


def solution(mesh):
    in_specs = (
        P(("groups", "cent", "sub"), None),
        P(("cent", "sub"), ("groups", "docs"), None),
        P(("cent", "sub"), ("groups", "docs")),
        P(("cent", "sub"), ("groups", "docs")),
        P(("cent", "sub"), None),
        P(),
        P(("groups", "docs"), None),
        P(),
        P(),
        P(),
        P(),
        P(),
        P(),
        P(),
        P(),
        P(),
    )
    out_specs = P(("groups", "docs"), ("cent", "sub"), None)
    return jax.shard_map(
        on_device, mesh=mesh, in_specs=in_specs, out_specs=out_specs, check_vma=False
    )
```
